32 devices in a mesh: groups: 2 (over y), expert: 4 (over z), dp: 4 (over x, core).
Axes of the slice: x: 2, y: 2, z: 4, core: 2. Of those that a mesh axis runs over, the one named last changes fastest.
Arguments:
- tokens: bfloat16 [1024, 2048], P(('groups', 'expert', 'dp')), parts along dimension 0, may hold values from -6 to 6
- out_grad: bfloat16 [1024, 2048], P(('groups', 'expert', 'dp')), parts along dimension 0, may hold values from -6 to 6
- expert_ids: int32 [1024, 8], P(('groups', 'expert', 'dp')), parts along dimension 0, may hold values from 0 to 15, as said below
- slot_pos: int32 [1024, 8], P(('groups', 'expert', 'dp')), parts along dimension 0, may hold values from -1 to 15, as said below
- combine_weight: float32 [1024, 8], P(('groups', 'expert', 'dp')), parts along dimension 0, may hold values from 0.05 to 0.6
- w_gate: bfloat16 [768, 16, 2048], P('dp', 'expert'), may hold values from -0.125 to 0.125
- w_up: bfloat16 [768, 16, 2048], P('dp', 'expert'), may hold values from -0.125 to 0.125
- w_down: bfloat16 [768, 16, 2048], P('dp', 'expert'), may hold values from -0.21875 to 0.21875
Outputs:
- layer_out: bfloat16 [1024, 2048], P(('groups', 'expert', 'dp')), parts along dimension 0
- input_grad: bfloat16 [1024, 2048], P(('groups', 'expert', 'dp')), parts along dimension 0
- weight_grad: float32 [1024, 8], P(('groups', 'expert', 'dp')), parts along dimension 0
- down_grad: bfloat16 [1536, 16, 2048], P(('groups', 'dp'), 'expert'), parts along dimension 0
The draws below stay inside these ranges and needn't reach their ends.
There are 2 independent parts, one for each index of `groups`. The reference program is written for one: setup_inputs(seed, part) draws one part's arguments, and reference() takes and returns one part's arrays. A program takes and returns all parts, laid end to end along the dimension named above; an argument that names none is the same for every part. Nothing has to cross between parts.
Inputs may be any that keep to these rules, and one draw needn't show every extreme that they name: `expert_ids`: each row names 8 different experts. In every aligned block of 32 rows one expert, the same for all blocks, is named by at least 17 rows. `slot_pos`: within each aligned block of 32 rows, the entries that name one expert hold distinct slots 0, 1, 2 and so on in a seeded priority order, and those past the first 16 hold -1; so every block fills all 16 slots of one expert and drops at least one entry.
All inputs are finite; a program needn't handle non-finite values.
Results may differ from the reference program's by a relative error of at most 0.009.
Values may be sent and summed in bfloat16 or wider, within the bound.
No kernel may reach another device: no remote copies, remote signals or barrier semaphores. Data moves between devices by JAX's collectives and lax.ppermute only.
A program may use at most 192 MiB of HBM per device.

```python
import math
import jax
import jax.numpy as jnp
from jax import lax

D = 2048
FF = 768
TOP = 8
TOK_DEV = 32
EXPERTS = 16
CAP = 16
TOKENS = 512
N_EXPERT = 4
N_DP = 4


def count_ahead(operand):
    block_ids, block_prio = operand
    earlier = (block_ids[:, None] == block_ids[None, :]) & (block_prio[None, :] < block_prio[:, None])
    return jnp.sum(earlier.astype(jnp.int32), axis=1)


def routing(key):
    block_total = TOKENS // TOK_DEV
    entry_total = TOK_DEV * TOP
    key_pick, key_hot, key_start, key_rank = jax.random.split(key, 4)
    scores = jax.random.randint(key_pick, (TOKENS, EXPERTS), 0, 1 << 20)
    scores = scores * EXPERTS + jnp.arange(EXPERTS, dtype=jnp.int32)[None, :]
    picked = lax.top_k(scores, TOP)[1].astype(jnp.int32)
    hottest = jax.random.randint(key_hot, (), 0, EXPERTS)
    offsets = jax.random.randint(key_start, (block_total,), 0, TOK_DEV)
    position = jnp.arange(TOKENS, dtype=jnp.int32)
    within = (position % TOK_DEV + offsets[position // TOK_DEV]) % TOK_DEV
    forced = within < CAP + 1
    shifted = (picked - picked[:, :1] + hottest) % EXPERTS
    expert_ids = jnp.where(forced[:, None], shifted, picked).astype(jnp.int32)
    priority = jax.random.randint(key_rank, (block_total, entry_total), 0, 1 << 16) * entry_total
    priority = priority + jnp.arange(entry_total, dtype=jnp.int32)[None, :]
    grouped = expert_ids.reshape(block_total, entry_total)
    ahead = lax.map(count_ahead, (grouped, priority)).reshape(TOKENS, TOP)
    slot_values = jnp.where(ahead < CAP, ahead, -1).astype(jnp.int32)
    return (expert_ids, slot_values)


def draw_expert_ids(key, part):
    return routing(key)[0]


def draw_slot_pos(key, part):
    return routing(key)[1]


def steps_of(rng, shape, shards, least, high):
    def one(dim, parts):
        draws = jax.random.uniform(jax.random.fold_in(jax.random.fold_in(rng, 6), dim), (parts,), jnp.float32, least / len(shards), high / len(shards))
        return jnp.repeat(jnp.exp(draws), shape[dim] // parts).reshape((-1,) + (1,) * (len(shape) - dim - 1))

    factor_of = one(*shards[0])
    for cut in shards[1:]:
        factor_of = factor_of * one(*cut)
    return factor_of


def centred(rng, extent, spread, reach, cuts=(), held_as=jnp.bfloat16):
    entries = jax.random.normal(rng, extent, jnp.float32) * spread
    if len(cuts) > 0:
        entries = steps_of(rng, extent, cuts, -0.22, 0.18) * entries
    return jnp.clip(entries, min=-reach, max=reach).astype(held_as)


def setup_inputs(seed: int = 0, part: int = 0) -> dict:
    arg_keys = jax.random.split(jax.random.key(seed), 9)
    part_splits = jax.random.split(jax.random.fold_in(arg_keys[8], part), 9)
    tokens = centred(part_splits[0], (TOKENS, D), 1.0, 6.0, ((0, 16),))
    out_grad = centred(part_splits[1], (TOKENS, D), 1.0, 6.0, ((0, 16),))
    expert_ids = draw_expert_ids(jax.random.fold_in(jax.random.fold_in(arg_keys[8], part), 71), part)
    slot_pos = draw_slot_pos(jax.random.fold_in(jax.random.fold_in(arg_keys[8], part), 71), part)
    combine_weight = jnp.clip(jnp.exp(math.log(0.6) - 2.4849067 * jax.random.uniform(part_splits[4], (TOKENS, TOP), jnp.float32) ** steps_of(part_splits[4], (TOKENS, TOP), ((0, 16),), -0.2, 0.2)), 0.05, 0.6)
    w_gate = centred(arg_keys[5], (FF, EXPERTS, D), D ** -0.5, 0.125, ((0, 4), (1, 4)))
    w_up = centred(arg_keys[6], (FF, EXPERTS, D), D ** -0.5, 0.125, ((0, 4), (1, 4)))
    w_down = centred(arg_keys[7], (FF, EXPERTS, D), FF ** -0.5, 0.21875, ((0, 4), (1, 4)))
    return dict(tokens=tokens, out_grad=out_grad, expert_ids=expert_ids, slot_pos=slot_pos, combine_weight=combine_weight, w_gate=w_gate, w_up=w_up, w_down=w_down)


def expert_pass(operands):
    slot_rows, slot_cot, gate_w, up_w, down_w = operands
    gate_pre = jnp.dot(slot_rows, gate_w.T, preferred_element_type=jnp.float32)
    up_pre = jnp.dot(slot_rows, up_w.T, preferred_element_type=jnp.float32)
    sigmoid_val = jax.nn.sigmoid(gate_pre)
    hidden = (gate_pre * sigmoid_val * up_pre).astype(jnp.bfloat16)
    expert_out = jnp.dot(hidden, down_w, preferred_element_type=jnp.float32).astype(jnp.bfloat16)
    hidden_grad = jnp.dot(slot_cot, down_w.T, preferred_element_type=jnp.float32)
    gate_grad = (hidden_grad * up_pre * sigmoid_val * (1.0 + gate_pre * (1.0 - sigmoid_val))).astype(jnp.bfloat16)
    up_grad = (hidden_grad * gate_pre * sigmoid_val).astype(jnp.bfloat16)
    slot_grad = jnp.dot(gate_grad, gate_w, preferred_element_type=jnp.float32)
    slot_grad = (slot_grad + jnp.dot(up_grad, up_w, preferred_element_type=jnp.float32)).astype(jnp.bfloat16)
    hidden_share = hidden.reshape(N_EXPERT, N_DP, CAP, FF).astype(jnp.float32)
    cot_share = slot_cot.reshape(N_EXPERT, N_DP, CAP, D).astype(jnp.float32)
    share_sum = jnp.einsum("sqcf,sqcd->qfd", hidden_share, cot_share, precision=lax.Precision.HIGHEST)
    share_sum = lax.optimization_barrier(share_sum.astype(jnp.bfloat16)).astype(jnp.float32)
    down_grad = jnp.sum(share_sum, axis=0).astype(jnp.bfloat16)
    return expert_out, slot_grad, down_grad


def reference(tokens, out_grad, expert_ids, slot_pos, combine_weight, w_gate, w_up, w_down):
    block_total = TOKENS // TOK_DEV
    kept_mask = slot_pos >= 0
    block_index = jnp.broadcast_to((jnp.arange(TOKENS, dtype=jnp.int32) // TOK_DEV)[:, None], (TOKENS, TOP)).astype(jnp.int32)
    slot_place = jnp.where(kept_mask, slot_pos, CAP).astype(jnp.int32)
    slot_cot = (combine_weight[:, :, None] * out_grad.astype(jnp.float32)[:, None, :]).astype(jnp.bfloat16)
    token_copies = jnp.broadcast_to(tokens[:, None, :], (TOKENS, TOP, D))
    row_table = jnp.zeros((EXPERTS, block_total, CAP, D), jnp.bfloat16)
    row_table = row_table.at[expert_ids, block_index, slot_place].set(token_copies, mode="drop")
    cot_table = jnp.zeros((EXPERTS, block_total, CAP, D), jnp.bfloat16)
    cot_table = cot_table.at[expert_ids, block_index, slot_place].set(slot_cot, mode="drop")
    operands = (
        row_table.reshape(EXPERTS, block_total * CAP, D),
        cot_table.reshape(EXPERTS, block_total * CAP, D),
        jnp.moveaxis(w_gate, 1, 0),
        jnp.moveaxis(w_up, 1, 0),
        jnp.moveaxis(w_down, 1, 0),
    )
    expert_out, slot_grad, down_grad = lax.map(expert_pass, operands)
    read_place = jnp.where(kept_mask, slot_pos, 0).astype(jnp.int32)
    picked_out = expert_out.reshape(EXPERTS, block_total, CAP, D)[expert_ids, block_index, read_place]
    picked_out = jnp.where(kept_mask[:, :, None], picked_out.astype(jnp.float32), jnp.float32(0.0))
    picked_grad = slot_grad.reshape(EXPERTS, block_total, CAP, D)[expert_ids, block_index, read_place]
    picked_grad = jnp.where(kept_mask[:, :, None], picked_grad.astype(jnp.float32), jnp.float32(0.0))
    layer_out = jnp.sum(combine_weight[:, :, None] * picked_out, axis=1).astype(jnp.bfloat16)
    input_grad = jnp.sum(picked_grad, axis=1).astype(jnp.bfloat16)
    weight_grad = jnp.sum(picked_out * out_grad.astype(jnp.float32)[:, None, :], axis=2)
    return (layer_out, input_grad, weight_grad, jnp.moveaxis(down_grad, 0, 1))
```

```python
import jax
import jax.numpy as jnp
from jax import lax
from jax.sharding import PartitionSpec as P


def slot_places(expert_ids, slot_pos, local_experts, row_total, capacity):
    flat_place = (
        expert_ids % local_experts * row_total + expert_ids // local_experts * capacity + slot_pos
    )
    return jnp.where(slot_pos >= 0, flat_place, -1)


def local(tokens, out_grad, expert_ids, slot_pos, combine_weight, w_gate, w_up, w_down):
    local_experts = w_gate.shape[1]
    expert_peers = lax.axis_size("expert")
    tok_count = tokens.shape[0]
    top_count = expert_ids.shape[1]
    model_width = tokens.shape[1]
    capacity = tok_count * top_count // (local_experts * expert_peers)
    row_total = expert_peers * capacity
    slot_count = local_experts * row_total
    kept_mask = slot_pos >= 0
    flat_place = slot_places(expert_ids, slot_pos, local_experts, row_total, capacity)
    places = jnp.arange(slot_count, dtype=jnp.int32)
    onehot = (flat_place[:, :, None] == places[None, None, :]).astype(jnp.float32)
    present = jnp.sum(onehot, axis=1)
    weighted = jnp.sum(onehot * combine_weight[:, :, None], axis=1)
    sent_rows = jnp.einsum(
        "tw,td->wd", present.astype(jnp.bfloat16), tokens, preferred_element_type=jnp.float32
    )
    sent_cot = jnp.einsum(
        "tw,td->wd", weighted, out_grad.astype(jnp.float32), precision=lax.Precision.HIGHEST
    )
    sent_rows = sent_rows.astype(jnp.bfloat16).reshape(local_experts, row_total, model_width)
    sent_cot = sent_cot.astype(jnp.bfloat16).reshape(local_experts, row_total, model_width)
    expert_rows, expert_cot = (
        lax.all_to_all(sent_rows, "expert", split_axis=1, concat_axis=1, tiled=True),
        lax.all_to_all(sent_cot, "expert", split_axis=1, concat_axis=1, tiled=True),
    )
    gate_piece = lax.all_gather(w_gate, "dp", axis=0, tiled=True)
    up_piece = lax.all_gather(w_up, "dp", axis=0, tiled=True)
    down_piece = lax.all_gather(w_down, "dp", axis=0, tiled=True)
    gate_pre = jnp.einsum(
        "nld,lrd->lnr", gate_piece, expert_rows, preferred_element_type=jnp.float32
    )
    up_pre = jnp.einsum("nld,lrd->lnr", up_piece, expert_rows, preferred_element_type=jnp.float32)
    sigmoid_val = jax.nn.sigmoid(gate_pre)
    hidden = (gate_pre * sigmoid_val * up_pre).astype(jnp.bfloat16)
    expert_out = jnp.einsum("lnr,nld->lrd", hidden, down_piece, preferred_element_type=jnp.float32)
    hidden_grad = jnp.einsum(
        "nld,lrd->lnr", down_piece, expert_cot, preferred_element_type=jnp.float32
    )
    gate_grad = (
        hidden_grad * up_pre * sigmoid_val * (1.0 + gate_pre * (1.0 - sigmoid_val))
    ).astype(jnp.bfloat16)
    up_grad = (hidden_grad * gate_pre * sigmoid_val).astype(jnp.bfloat16)
    slot_back = jnp.einsum(
        "lnr,nld->lrd", gate_grad, gate_piece, preferred_element_type=jnp.float32
    )
    slot_back = slot_back + jnp.einsum(
        "lnr,nld->lrd", up_grad, up_piece, preferred_element_type=jnp.float32
    )
    hidden_all, expert_out, slot_back = (hidden, expert_out, slot_back)
    back_out, back_grad = (
        lax.all_to_all(
            expert_out.astype(jnp.bfloat16), "expert", split_axis=1, concat_axis=1, tiled=True
        ),
        lax.all_to_all(
            slot_back.astype(jnp.bfloat16), "expert", split_axis=1, concat_axis=1, tiled=True
        ),
    )
    back_out = back_out.reshape(slot_count, model_width)
    back_grad = back_grad.reshape(slot_count, model_width)
    safe_place = jnp.maximum(flat_place, 0)
    picked_out = jnp.where(
        kept_mask[:, :, None], jnp.take(back_out, safe_place, axis=0).astype(jnp.float32), 0.0
    )
    picked_grad = jnp.where(
        kept_mask[:, :, None], jnp.take(back_grad, safe_place, axis=0).astype(jnp.float32), 0.0
    )
    layer_out = jnp.sum(combine_weight[:, :, None] * picked_out, axis=1).astype(jnp.bfloat16)
    input_grad = jnp.sum(picked_grad, axis=1).astype(jnp.bfloat16)
    weight_grad = jnp.sum(picked_out * out_grad.astype(jnp.float32)[:, None, :], axis=2)
    down_grad = lax.psum_scatter(
        jnp.einsum(
            "lnr,lrd->nld", hidden_all, expert_cot, preferred_element_type=jnp.float32
        ).astype(jnp.bfloat16),
        "dp",
        scatter_dimension=0,
        tiled=True,
    )
    return (layer_out, input_grad, weight_grad, down_grad)


def hypercube(size):
    return [1 << bit for bit in range(size.bit_length() - 1)]


def gather_rows(rows):
    expert_peers = lax.axis_size("expert")
    dp_peers = lax.axis_size("dp")
    pieces = [rows]
    for shift in range(1, expert_peers):
        pairs = [(i, (i + shift) % expert_peers) for i in range(expert_peers)]
        pieces.append(lax.ppermute(rows, "expert", pairs))
    held = jnp.concatenate(pieces, axis=0)
    for bit in reversed(hypercube(dp_peers)):
        other = lax.ppermute(held, "dp", [(i, i ^ bit) for i in range(dp_peers)])
        held = jnp.concatenate([held, other], axis=0)
    return held


def scatter_sum(part):
    expert_peers = lax.axis_size("expert")
    dp_peers = lax.axis_size("dp")
    for bit in hypercube(dp_peers):
        half = part.shape[0] // 2
        sent = part[half:].astype(jnp.bfloat16)
        other = lax.ppermute(sent, "dp", [(i, i ^ bit) for i in range(dp_peers)])
        part = part[:half].astype(jnp.float32) + other.astype(jnp.float32)
    block = part.shape[0] // expert_peers
    total = part[:block]
    for shift in range(1, expert_peers):
        pairs = [(i, (i - shift) % expert_peers) for i in range(expert_peers)]
        sent = part[shift * block : (shift + 1) * block].astype(jnp.bfloat16)
        total = total + lax.ppermute(sent, "expert", pairs).astype(jnp.float32)
    return total


def dot_last(a, b):
    return lax.dot_general(a, b, (((1,), (1,)), ((), ())), preferred_element_type=jnp.float32)


def dot_plain(a, b):
    return lax.dot_general(a, b, (((1,), (0,)), ((), ())), preferred_element_type=jnp.float32)


def dot_first(a, b):
    return lax.dot_general(a, b, (((0,), (0,)), ((), ())), preferred_element_type=jnp.float32)


def local_tokens(tokens, out_grad, expert_ids, slot_pos, combine_weight, w_gate, w_up, w_down):
    units, local_experts, width = w_gate.shape
    experts = local_experts * lax.axis_size("expert")
    first_expert = lax.axis_index("expert") * local_experts
    picked = (expert_ids[:, :, None] == jnp.arange(experts, dtype=jnp.int32)) & (slot_pos >= 0)[:, :, None]
    weight = jnp.sum(jnp.where(picked, combine_weight[:, :, None], 0.0), axis=1)
    high = lax.reduce_precision(weight, 8, 7)
    side = -(-2 * experts // 128) * 128
    routed = jnp.concatenate([high, weight - high], axis=1).astype(jnp.bfloat16)
    routed = jnp.pad(routed, ((0, 0), (0, side - 2 * experts)))

    token_rows = gather_rows(jnp.concatenate([tokens, routed], axis=1))
    grad_rows = gather_rows(out_grad)
    weight_rows = token_rows[:, width:]
    token_rows = token_rows[:, :width]

    unit_rows = units * local_experts
    gate_w = w_gate.reshape(unit_rows, width)
    up_w = w_up.reshape(unit_rows, width)
    down_w = w_down.reshape(unit_rows, width)
    unit_expert = first_expert + jnp.arange(unit_rows, dtype=jnp.int32) % local_experts
    columns = jnp.arange(side, dtype=jnp.int32)
    spread = (columns[:, None] % experts == unit_expert[None, :]) & (columns < 2 * experts)[:, None]
    collect = (unit_expert[:, None] == columns[None, :]).astype(jnp.bfloat16)
    mask = dot_plain(weight_rows, spread.astype(jnp.bfloat16))

    gate_pre = dot_last(token_rows, gate_w)
    up_pre = dot_last(token_rows, up_w)
    sig = jax.nn.sigmoid(gate_pre)
    hidden = gate_pre * sig * up_pre
    hidden_weighted = (hidden * mask).astype(jnp.bfloat16)
    out_part = dot_plain(hidden_weighted, down_w).astype(jnp.bfloat16)
    layer_out = scatter_sum(out_part).astype(jnp.bfloat16)

    hidden_grad = dot_last(grad_rows, down_w)
    product = jnp.where(mask > 0, hidden * hidden_grad, 0.0).astype(jnp.bfloat16)
    product_part = dot_plain(product, collect).astype(jnp.bfloat16)
    hidden_grad = hidden_grad * mask
    gate_grad = (hidden_grad * up_pre * sig * (1.0 + gate_pre * (1.0 - sig))).astype(jnp.bfloat16)
    up_grad = (hidden_grad * gate_pre * sig).astype(jnp.bfloat16)
    grad_part = (dot_plain(gate_grad, gate_w) + dot_plain(up_grad, up_w)).astype(jnp.bfloat16)
    sums = scatter_sum(jnp.concatenate([grad_part, product_part], axis=1))
    input_grad = sums[:, :width].astype(jnp.bfloat16)
    per_expert = sums[:, width : width + experts]
    weight_grad = jnp.sum(jnp.where(picked, per_expert[:, None, :], 0.0), axis=2)
    down_grad = dot_first(hidden_weighted, grad_rows).astype(jnp.bfloat16)
    return (layer_out, input_grad, weight_grad, down_grad.reshape(units, local_experts, width))


def plan(tokens, out_grad, expert_ids, slot_pos, combine_weight, w_gate, w_up, w_down):
    args = (tokens, out_grad, expert_ids, slot_pos, combine_weight, w_gate, w_up, w_down)
    slots = tokens.shape[0] * expert_ids.shape[1] // lax.axis_size("expert")
    dp_peers = lax.axis_size("dp")
    if tokens.shape[0] < slots and dp_peers & (dp_peers - 1) == 0:
        return local_tokens(*args)
    return local(*args)


def solution(mesh):
    in_specs = (
        P(("groups", "expert", "dp"), None),
        P(("groups", "expert", "dp"), None),
        P(("groups", "expert", "dp"), None),
        P(("groups", "expert", "dp"), None),
        P(("groups", "expert", "dp"), None),
        P("dp", "expert", None),
        P("dp", "expert", None),
        P("dp", "expert", None),
    )
    out_specs = (
        P(("groups", "expert", "dp"), None),
        P(("groups", "expert", "dp"), None),
        P(("groups", "expert", "dp"), None),
        P(("groups", "dp"), "expert", None),
    )
    return jax.shard_map(plan, mesh=mesh, in_specs=in_specs, out_specs=out_specs, check_vma=False)
```

```python
import jax
import jax.numpy as jnp
from jax import lax
from jax.experimental import pallas as pl
from jax.experimental.pallas import tpu as pltpu
from jax.sharding import PartitionSpec as P


def slot_places(expert_ids, slot_pos, local_experts, row_total, capacity):
    flat_place = (
        expert_ids % local_experts * row_total + expert_ids // local_experts * capacity + slot_pos
    )
    return jnp.where(slot_pos >= 0, flat_place, -1)


def local(tokens, out_grad, expert_ids, slot_pos, combine_weight, w_gate, w_up, w_down):
    local_experts = w_gate.shape[1]
    expert_peers = lax.axis_size("expert")
    tok_count = tokens.shape[0]
    top_count = expert_ids.shape[1]
    model_width = tokens.shape[1]
    capacity = tok_count * top_count // (local_experts * expert_peers)
    row_total = expert_peers * capacity
    slot_count = local_experts * row_total
    kept_mask = slot_pos >= 0
    flat_place = slot_places(expert_ids, slot_pos, local_experts, row_total, capacity)
    places = jnp.arange(slot_count, dtype=jnp.int32)
    onehot = (flat_place[:, :, None] == places[None, None, :]).astype(jnp.float32)
    present = jnp.sum(onehot, axis=1)
    weighted = jnp.sum(onehot * combine_weight[:, :, None], axis=1)
    sent_rows = jnp.einsum(
        "tw,td->wd", present.astype(jnp.bfloat16), tokens, preferred_element_type=jnp.float32
    )
    sent_cot = jnp.einsum(
        "tw,td->wd", weighted, out_grad.astype(jnp.float32), precision=lax.Precision.HIGHEST
    )
    sent_rows = sent_rows.astype(jnp.bfloat16).reshape(local_experts, row_total, model_width)
    sent_cot = sent_cot.astype(jnp.bfloat16).reshape(local_experts, row_total, model_width)
    expert_rows, expert_cot = (
        lax.all_to_all(sent_rows, "expert", split_axis=1, concat_axis=1, tiled=True),
        lax.all_to_all(sent_cot, "expert", split_axis=1, concat_axis=1, tiled=True),
    )
    gate_piece = lax.all_gather(w_gate, "dp", axis=0, tiled=True)
    up_piece = lax.all_gather(w_up, "dp", axis=0, tiled=True)
    down_piece = lax.all_gather(w_down, "dp", axis=0, tiled=True)
    gate_pre = jnp.einsum(
        "nld,lrd->lnr", gate_piece, expert_rows, preferred_element_type=jnp.float32
    )
    up_pre = jnp.einsum("nld,lrd->lnr", up_piece, expert_rows, preferred_element_type=jnp.float32)
    sigmoid_val = jax.nn.sigmoid(gate_pre)
    hidden = (gate_pre * sigmoid_val * up_pre).astype(jnp.bfloat16)
    expert_out = jnp.einsum("lnr,nld->lrd", hidden, down_piece, preferred_element_type=jnp.float32)
    hidden_grad = jnp.einsum(
        "nld,lrd->lnr", down_piece, expert_cot, preferred_element_type=jnp.float32
    )
    gate_grad = (
        hidden_grad * up_pre * sigmoid_val * (1.0 + gate_pre * (1.0 - sigmoid_val))
    ).astype(jnp.bfloat16)
    up_grad = (hidden_grad * gate_pre * sigmoid_val).astype(jnp.bfloat16)
    slot_back = jnp.einsum(
        "lnr,nld->lrd", gate_grad, gate_piece, preferred_element_type=jnp.float32
    )
    slot_back = slot_back + jnp.einsum(
        "lnr,nld->lrd", up_grad, up_piece, preferred_element_type=jnp.float32
    )
    hidden_all, expert_out, slot_back = (hidden, expert_out, slot_back)
    back_out, back_grad = (
        lax.all_to_all(
            expert_out.astype(jnp.bfloat16), "expert", split_axis=1, concat_axis=1, tiled=True
        ),
        lax.all_to_all(
            slot_back.astype(jnp.bfloat16), "expert", split_axis=1, concat_axis=1, tiled=True
        ),
    )
    back_out = back_out.reshape(slot_count, model_width)
    back_grad = back_grad.reshape(slot_count, model_width)
    safe_place = jnp.maximum(flat_place, 0)
    picked_out = jnp.where(
        kept_mask[:, :, None], jnp.take(back_out, safe_place, axis=0).astype(jnp.float32), 0.0
    )
    picked_grad = jnp.where(
        kept_mask[:, :, None], jnp.take(back_grad, safe_place, axis=0).astype(jnp.float32), 0.0
    )
    layer_out = jnp.sum(combine_weight[:, :, None] * picked_out, axis=1).astype(jnp.bfloat16)
    input_grad = jnp.sum(picked_grad, axis=1).astype(jnp.bfloat16)
    weight_grad = jnp.sum(picked_out * out_grad.astype(jnp.float32)[:, None, :], axis=2)
    down_grad = lax.psum_scatter(
        jnp.einsum(
            "lnr,lrd->nld", hidden_all, expert_cot, preferred_element_type=jnp.float32
        ).astype(jnp.bfloat16),
        "dp",
        scatter_dimension=0,
        tiled=True,
    )
    return (layer_out, input_grad, weight_grad, down_grad)


def over_z(rows, shift):
    peers = lax.axis_size("expert")
    return lax.ppermute(rows, "expert", [(i, (i + shift) % peers) for i in range(peers)])


def over_dp(rows, bit):
    return lax.ppermute(rows, "dp", [(i, i ^ bit) for i in range(lax.axis_size("dp"))])


def after(value, *others):
    return lax.optimization_barrier((value,) + others)[0]


def add(kept, other):
    return kept.astype(jnp.float32) + other.astype(jnp.float32)


def narrow(rows):
    return rows.astype(jnp.bfloat16)


def cross_x(part):
    block = part.shape[0] // 8
    far_x = over_dp(part[7 * block :], 2)
    rest_x = over_dp(part[4 * block : 7 * block], 2)
    far = narrow(add(part[3 * block : 4 * block], far_x))
    rest = add(part[: 3 * block], rest_x)
    return rest[:block], narrow(rest[block : 2 * block]), narrow(rest[2 * block :]), far


def cross_z(own, near_left, near_right, far):
    far_sum = over_z(far, -2)
    left, right = over_z(near_left, -1), over_z(near_right, -3)
    return add(own, far_sum) + add(left, right)


def dot_last(a, b):
    return lax.dot_general(a, b, (((1,), (1,)), ((), ())), preferred_element_type=jnp.float32)


def dot_plain(a, b):
    return lax.dot_general(a, b, (((1,), (0,)), ((), ())), preferred_element_type=jnp.float32)


def dot_first(a, b):
    return lax.dot_general(a, b, (((0,), (0,)), ((), ())), preferred_element_type=jnp.float32)


UNIT_TILE = 256
WIDTH_TILE = 512


def place_rows(pieces, rows):
    start = 0
    for piece in pieces:
        count = piece.shape[0]
        rows[pl.ds(start, count), :] = piece[...]
        start += count


def forward_kernel(spread, collect, *refs):
    del collect
    pieces, refs = refs[:5], refs[5:]
    gate_a, gate_b, up_a, up_b, down_a, down_b, out, gate_out, up_out, mask, weighted, rows = refs
    step = pl.program_id(0)
    tiles = weighted.shape[1] // UNIT_TILE
    features = gate_a.shape[1]

    @pl.when(step == 0)
    def _():
        place_rows(pieces, rows)
        mask[...] = dot_plain(rows[:, features:], spread[...])

    def units(gate_w, up_w):
        token_rows = rows[:, :features]
        gate_pre = dot_last(token_rows, gate_w[...])
        up_pre = dot_last(token_rows, up_w[...])
        gate_out[...] = gate_pre
        up_out[...] = up_pre
        hidden = gate_pre * jax.nn.sigmoid(gate_pre) * up_pre
        at = pl.multiple_of(step * UNIT_TILE, UNIT_TILE)
        weighted[:, pl.ds(at, UNIT_TILE)] = (hidden * mask[...]).astype(jnp.bfloat16)

    @pl.when(step < tiles // 2)
    def _():
        units(gate_a, up_a)

    @pl.when((step >= tiles // 2) & (step < tiles))
    def _():
        units(gate_b, up_b)

    @pl.when(step >= tiles)
    def _():
        half = down_a.shape[0]
        total = dot_plain(weighted[:, :half], down_a[...]) + dot_plain(weighted[:, half:], down_b[...])
        out[...] = total.astype(jnp.bfloat16)


def backward_kernel(spread, collect, *refs):
    del spread
    pieces, refs = refs[:6], refs[6:]
    gate_a, gate_b, up_a, up_b, down_a, down_b, gate_in, up_in, mask, out, product_out, rows, gate_grad, up_grad, product = refs
    step = pl.program_id(0)
    tiles = gate_grad.shape[1] // UNIT_TILE

    @pl.when(step == 0)
    def _():
        place_rows(pieces, rows)
        product[...] = jnp.zeros_like(product)

    def units(down_w):
        hidden_grad = dot_last(rows[...], down_w[...])
        gate_pre, up_pre, weight = gate_in[...], up_in[...], mask[...]
        sig = jax.nn.sigmoid(gate_pre)
        gate_sig = gate_pre * sig
        product[...] += jnp.where(weight > 0, gate_sig * up_pre * hidden_grad, 0.0)
        hidden_grad = hidden_grad * weight
        at = pl.multiple_of(step * UNIT_TILE, UNIT_TILE)
        slope = sig * (1.0 + gate_pre * (1.0 - sig))
        gate_grad[:, pl.ds(at, UNIT_TILE)] = (hidden_grad * up_pre * slope).astype(jnp.bfloat16)
        up_grad[:, pl.ds(at, UNIT_TILE)] = (hidden_grad * gate_sig).astype(jnp.bfloat16)

    @pl.when(step < tiles // 2)
    def _():
        units(down_a)

    @pl.when((step >= tiles // 2) & (step < tiles))
    def _():
        units(down_b)

    @pl.when(step == tiles)
    def _():
        product_out[...] = dot_plain(product[...].astype(jnp.bfloat16), collect[...]).astype(jnp.bfloat16)

    @pl.when(step >= tiles)
    def _():
        half = gate_a.shape[0]
        total = dot_plain(gate_grad[:, :half], gate_a[...]) + dot_plain(gate_grad[:, half:], gate_b[...])
        total += dot_plain(up_grad[:, :half], up_a[...]) + dot_plain(up_grad[:, half:], up_b[...])
        out[...] = total.astype(jnp.bfloat16)


def merge_kernel(gate, up, down, merged):
    for slot, part in enumerate((gate, up, down)):
        merged[slot] = part[...].reshape(merged.shape[1:])


def merge_units(gate, up, down):
    units, experts, features = gate.shape
    tile = 32
    block = pl.BlockSpec((tile, experts, features), lambda i: (i, 0, 0))
    return pl.pallas_call(
        merge_kernel,
        grid=(units // tile,),
        in_specs=[block] * 3,
        out_specs=pl.BlockSpec((3, tile * experts, features), lambda i: (0, i, 0)),
        out_shape=jax.ShapeDtypeStruct((3, units * experts, features), gate.dtype),
        compiler_params=pltpu.CompilerParams(**PARAMS),
        cost_estimate=pl.CostEstimate(flops=0, bytes_accessed=12 * gate.size, transcendentals=0),
        name="merge_units",
    )(gate, up, down)


def whole(array):
    return pl.BlockSpec(array.shape, lambda i: (0, 0))


def by_units(array, slot, first):
    last = array.shape[1] // UNIT_TILE - 1
    return pl.BlockSpec((None, UNIT_TILE, array.shape[2]), lambda i: (slot, jnp.clip(i - first, 0, last), 0))


def by_width(array, slot, first):
    return pl.BlockSpec((None, array.shape[1], WIDTH_TILE), lambda i: (slot, 0, jnp.maximum(i - first, 0)))


def unit_columns(rows, tiles):
    return pl.BlockSpec((rows, UNIT_TILE), lambda i: (0, jnp.minimum(i, tiles - 1)))


def width_columns(rows, tiles):
    return pl.BlockSpec((rows, WIDTH_TILE), lambda i: (0, jnp.maximum(i - tiles, 0)))


def cost(rows, units, features, products):
    return pl.CostEstimate(
        flops=2 * rows * units * features * products,
        bytes_accessed=6 * units * features + 4 * rows * features,
        transcendentals=rows * units,
    )


PARAMS = dict(dimension_semantics=("arbitrary",), vmem_limit_bytes=48 * 1024 * 1024)


def forward(tables, pieces, weights):
    half, features = weights[0].shape[1:]
    rows = sum(piece.shape[0] for piece in pieces)
    tiles = 2 * half // UNIT_TILE
    operands = [*tables, *pieces, *weights * 3]
    specs = [whole(x) for x in (*tables, *pieces)]
    specs += [by_units(w, slot, n * tiles // 2) for slot in range(2) for n, w in enumerate(weights)]
    specs += [by_width(w, 2, tiles) for w in weights]
    return pl.pallas_call(
        forward_kernel,
        grid=(tiles + features // WIDTH_TILE,),
        in_specs=specs,
        out_specs=[
            width_columns(rows, tiles),
            unit_columns(rows, tiles),
            unit_columns(rows, tiles),
            pl.BlockSpec((rows, UNIT_TILE), lambda i: (0, 0)),
            pl.BlockSpec((rows, 2 * half), lambda i: (0, 0)),
        ],
        out_shape=[
            jax.ShapeDtypeStruct((rows, features), jnp.bfloat16),
            jax.ShapeDtypeStruct((rows, 2 * half), jnp.float32),
            jax.ShapeDtypeStruct((rows, 2 * half), jnp.float32),
            jax.ShapeDtypeStruct((rows, UNIT_TILE), jnp.float32),
            jax.ShapeDtypeStruct((rows, 2 * half), jnp.bfloat16),
        ],
        scratch_shapes=[pltpu.VMEM((rows, pieces[0].shape[1]), jnp.bfloat16)],
        compiler_params=pltpu.CompilerParams(**PARAMS),
        cost_estimate=cost(rows, 2 * half, features, 3),
        name="forward_products",
    )(*operands)


def backward(tables, pieces, weights, gate_pre, up_pre, mask):
    half, features = weights[0].shape[1:]
    rows = sum(piece.shape[0] for piece in pieces)
    tiles = 2 * half // UNIT_TILE
    operands = [*tables, *pieces, *weights * 3, gate_pre, up_pre, mask]
    specs = [whole(x) for x in (*tables, *pieces)]
    specs += [by_width(w, slot, tiles) for slot in range(2) for w in weights]
    specs += [by_units(w, 2, n * tiles // 2) for n, w in enumerate(weights)]
    specs += [unit_columns(rows, tiles), unit_columns(rows, tiles), whole(mask)]
    side = tables[1].shape[1]
    return pl.pallas_call(
        backward_kernel,
        grid=(tiles + features // WIDTH_TILE,),
        in_specs=specs,
        out_specs=[
            width_columns(rows, tiles),
            pl.BlockSpec((rows, side), lambda i: (0, 0)),
            pl.BlockSpec((rows, features), lambda i: (0, 0)),
        ],
        out_shape=[
            jax.ShapeDtypeStruct((rows, features), jnp.bfloat16),
            jax.ShapeDtypeStruct((rows, side), jnp.bfloat16),
            jax.ShapeDtypeStruct((rows, features), jnp.bfloat16),
        ],
        scratch_shapes=[
            pltpu.VMEM((rows, 2 * half), jnp.bfloat16),
            pltpu.VMEM((rows, 2 * half), jnp.bfloat16),
            pltpu.VMEM((rows, UNIT_TILE), jnp.float32),
        ],
        compiler_params=pltpu.CompilerParams(**PARAMS),
        cost_estimate=cost(rows, 2 * half, features, 3),
        name="backward_products",
    )(*operands)


def share_kernel(weighted, rows, other, out):
    total = dot_first(weighted[...], rows[...]) + other[...].astype(jnp.float32)
    out[...] = total.astype(jnp.bfloat16).reshape(out.shape)


def finish_share(weighted, rows, other, local_experts):
    count, features = rows.shape
    units = other.shape[0] // local_experts
    tile = UNIT_TILE // local_experts
    return pl.pallas_call(
        share_kernel,
        grid=(units // tile,),
        in_specs=[
            pl.BlockSpec((count, UNIT_TILE), lambda i: (0, i)),
            whole(rows),
            pl.BlockSpec((UNIT_TILE, features), lambda i: (i, 0)),
        ],
        out_specs=pl.BlockSpec((tile, local_experts, features), lambda i: (i, 0, 0)),
        out_shape=jax.ShapeDtypeStruct((units, local_experts, features), jnp.bfloat16),
        compiler_params=pltpu.CompilerParams(**PARAMS),
        cost_estimate=pl.CostEstimate(
            flops=2 * count * other.size, bytes_accessed=4 * other.size, transcendentals=0
        ),
        name="finish_share",
    )(weighted, rows, other)


def local_tokens(tokens, out_grad, expert_ids, slot_pos, combine_weight, w_gate, w_up, w_down):
    units, local_experts, width = w_gate.shape
    experts = local_experts * lax.axis_size("expert")
    first_expert = lax.axis_index("expert") * local_experts
    unit_rows = units * local_experts
    picked = (expert_ids[:, :, None] == jnp.arange(experts, dtype=jnp.int32)) & (slot_pos >= 0)[:, :, None]
    weight = jnp.sum(jnp.where(picked, combine_weight[:, :, None], 0.0), axis=1)
    high = lax.reduce_precision(weight, 8, 7)
    side = -(-2 * experts // 128) * 128
    routed = jnp.concatenate([high, weight - high], axis=1).astype(jnp.bfloat16)
    routed = jnp.pad(routed, ((0, 0), (0, side - 2 * experts)))
    unit_expert = first_expert + jnp.arange(UNIT_TILE, dtype=jnp.int32) % local_experts
    columns = jnp.arange(side, dtype=jnp.int32)
    spread = (columns[:, None] % experts == unit_expert[None, :]) & (columns < 2 * experts)[:, None]
    collect = (unit_expert[:, None] == columns[None, :]).astype(jnp.bfloat16)
    tables = (spread.astype(jnp.bfloat16), collect)

    own_t = jnp.concatenate([tokens, routed], axis=1)
    own_t, own_g, w_gate = lax.optimization_barrier((own_t, out_grad, w_gate))
    column_t = [over_z(own_t, 1), over_z(own_t, 3), over_z(own_t, 2)]
    own_gx = over_dp(own_g, 2)
    weights = merge_units(w_gate, w_up, w_down)
    column_t, own_gx, own_g, weights = lax.optimization_barrier((column_t, own_gx, own_g, weights))

    pieces_t = [own_t, *column_t]
    column_tx = over_dp(jnp.concatenate(pieces_t, axis=0), 2)
    near_g = [over_z(own_g, 1), over_z(own_g, 3)]
    far_g = over_z(own_g, 2)
    weights_b = over_dp(weights, 1)
    near_g, far_g, column_tx = lax.optimization_barrier((near_g, far_g, column_tx))

    away_gx = over_dp(jnp.concatenate([*near_g, far_g], axis=0), 2)
    weights = [weights, weights_b]
    out_part, gate_pre, up_pre, mask, weighted = forward(tables, [*pieces_t, column_tx], weights)
    out_part, away_gx = lax.optimization_barrier((out_part, away_gx))
    out_pieces = cross_x(out_part)

    grad_pieces = [out_grad, *near_g, far_g, own_gx, away_gx]
    grad_part, product_part, grad_rows = backward(tables, grad_pieces, weights, gate_pre, up_pre, mask)
    grad_part = jnp.concatenate([grad_part, product_part], axis=1)
    grad_part, out_pieces, weighted_b = lax.optimization_barrier((grad_part, out_pieces, weighted[:, unit_rows:]))
    block = own_t.shape[0]
    far_x = over_dp(grad_part[7 * block :], 2)
    rest_x = over_dp(grad_part[4 * block : 7 * block], 2)
    share_b = narrow(dot_first(weighted_b, grad_rows))
    far_x, share_b = lax.optimization_barrier((far_x, share_b))
    other_share = over_dp(share_b, 1)
    far = narrow(add(grad_part[3 * block : 4 * block], far_x))
    far_sum = over_z(far, -2)
    layer_out = narrow(cross_z(*out_pieces))
    rest_x, other_share, layer_out = lax.optimization_barrier((rest_x, other_share, layer_out))
    rest = add(grad_part[: 3 * block], rest_x)
    left, right = over_z(narrow(rest[block : 2 * block]), -1), over_z(narrow(rest[2 * block :]), -3)
    down_grad = finish_share(weighted, grad_rows, other_share, local_experts)
    left, right, far_sum, down_grad = lax.optimization_barrier((left, right, far_sum, down_grad))
    sums = add(rest[:block], far_sum) + add(left, right)
    input_grad = narrow(sums[:, :width])
    per_expert = sums[:, width : width + experts]
    weight_grad = jnp.sum(jnp.where(picked, per_expert[:, None, :], 0.0), axis=2)
    return (layer_out, input_grad, weight_grad, down_grad)


def plan(tokens, out_grad, expert_ids, slot_pos, combine_weight, w_gate, w_up, w_down):
    args = (tokens, out_grad, expert_ids, slot_pos, combine_weight, w_gate, w_up, w_down)
    slots = tokens.shape[0] * expert_ids.shape[1] // lax.axis_size("expert")
    unit_rows = w_gate.shape[0] * w_gate.shape[1]
    tiled = w_gate.shape[0] % 64 == 0 and unit_rows % UNIT_TILE == 0 and UNIT_TILE % w_gate.shape[1] == 0
    tiled = tiled and w_gate.shape[2] % WIDTH_TILE == 0 and tokens.shape[0] % 32 == 0
    four = lax.axis_size("expert") == 4 and lax.axis_size("dp") == 4
    if tokens.shape[0] < slots and tiled and four:
        return local_tokens(*args)
    return local(*args)


def solution(mesh):
    in_specs = (
        P(("groups", "expert", "dp"), None),
        P(("groups", "expert", "dp"), None),
        P(("groups", "expert", "dp"), None),
        P(("groups", "expert", "dp"), None),
        P(("groups", "expert", "dp"), None),
        P("dp", "expert", None),
        P("dp", "expert", None),
        P("dp", "expert", None),
    )
    out_specs = (
        P(("groups", "expert", "dp"), None),
        P(("groups", "expert", "dp"), None),
        P(("groups", "expert", "dp"), None),
        P(("groups", "dp"), "expert", None),
    )
    return jax.shard_map(plan, mesh=mesh, in_specs=in_specs, out_specs=out_specs, check_vma=False)
```

```python
import jax
import jax.numpy as jnp
from jax import lax
from jax.experimental import pallas as pl
from jax.experimental.pallas import tpu as pltpu
from jax.sharding import PartitionSpec as P


def slot_places(expert_ids, slot_pos, local_experts, row_total, capacity):
    flat_place = (
        expert_ids % local_experts * row_total + expert_ids // local_experts * capacity + slot_pos
    )
    return jnp.where(slot_pos >= 0, flat_place, -1)


def local(tokens, out_grad, expert_ids, slot_pos, combine_weight, w_gate, w_up, w_down):
    local_experts = w_gate.shape[1]
    expert_peers = lax.axis_size("expert")
    tok_count = tokens.shape[0]
    top_count = expert_ids.shape[1]
    model_width = tokens.shape[1]
    capacity = tok_count * top_count // (local_experts * expert_peers)
    row_total = expert_peers * capacity
    slot_count = local_experts * row_total
    kept_mask = slot_pos >= 0
    flat_place = slot_places(expert_ids, slot_pos, local_experts, row_total, capacity)
    places = jnp.arange(slot_count, dtype=jnp.int32)
    onehot = (flat_place[:, :, None] == places[None, None, :]).astype(jnp.float32)
    present = jnp.sum(onehot, axis=1)
    weighted = jnp.sum(onehot * combine_weight[:, :, None], axis=1)
    sent_rows = jnp.einsum(
        "tw,td->wd", present.astype(jnp.bfloat16), tokens, preferred_element_type=jnp.float32
    )
    sent_cot = jnp.einsum(
        "tw,td->wd", weighted, out_grad.astype(jnp.float32), precision=lax.Precision.HIGHEST
    )
    sent_rows = sent_rows.astype(jnp.bfloat16).reshape(local_experts, row_total, model_width)
    sent_cot = sent_cot.astype(jnp.bfloat16).reshape(local_experts, row_total, model_width)
    expert_rows, expert_cot = (
        lax.all_to_all(sent_rows, "expert", split_axis=1, concat_axis=1, tiled=True),
        lax.all_to_all(sent_cot, "expert", split_axis=1, concat_axis=1, tiled=True),
    )
    gate_piece = lax.all_gather(w_gate, "dp", axis=0, tiled=True)
    up_piece = lax.all_gather(w_up, "dp", axis=0, tiled=True)
    down_piece = lax.all_gather(w_down, "dp", axis=0, tiled=True)
    gate_pre = jnp.einsum(
        "nld,lrd->lnr", gate_piece, expert_rows, preferred_element_type=jnp.float32
    )
    up_pre = jnp.einsum("nld,lrd->lnr", up_piece, expert_rows, preferred_element_type=jnp.float32)
    sigmoid_val = jax.nn.sigmoid(gate_pre)
    hidden = (gate_pre * sigmoid_val * up_pre).astype(jnp.bfloat16)
    expert_out = jnp.einsum("lnr,nld->lrd", hidden, down_piece, preferred_element_type=jnp.float32)
    hidden_grad = jnp.einsum(
        "nld,lrd->lnr", down_piece, expert_cot, preferred_element_type=jnp.float32
    )
    gate_grad = (
        hidden_grad * up_pre * sigmoid_val * (1.0 + gate_pre * (1.0 - sigmoid_val))
    ).astype(jnp.bfloat16)
    up_grad = (hidden_grad * gate_pre * sigmoid_val).astype(jnp.bfloat16)
    slot_back = jnp.einsum(
        "lnr,nld->lrd", gate_grad, gate_piece, preferred_element_type=jnp.float32
    )
    slot_back = slot_back + jnp.einsum(
        "lnr,nld->lrd", up_grad, up_piece, preferred_element_type=jnp.float32
    )
    hidden_all, expert_out, slot_back = (hidden, expert_out, slot_back)
    back_out, back_grad = (
        lax.all_to_all(
            expert_out.astype(jnp.bfloat16), "expert", split_axis=1, concat_axis=1, tiled=True
        ),
        lax.all_to_all(
            slot_back.astype(jnp.bfloat16), "expert", split_axis=1, concat_axis=1, tiled=True
        ),
    )
    back_out = back_out.reshape(slot_count, model_width)
    back_grad = back_grad.reshape(slot_count, model_width)
    safe_place = jnp.maximum(flat_place, 0)
    picked_out = jnp.where(
        kept_mask[:, :, None], jnp.take(back_out, safe_place, axis=0).astype(jnp.float32), 0.0
    )
    picked_grad = jnp.where(
        kept_mask[:, :, None], jnp.take(back_grad, safe_place, axis=0).astype(jnp.float32), 0.0
    )
    layer_out = jnp.sum(combine_weight[:, :, None] * picked_out, axis=1).astype(jnp.bfloat16)
    input_grad = jnp.sum(picked_grad, axis=1).astype(jnp.bfloat16)
    weight_grad = jnp.sum(picked_out * out_grad.astype(jnp.float32)[:, None, :], axis=2)
    down_grad = lax.psum_scatter(
        jnp.einsum(
            "lnr,lrd->nld", hidden_all, expert_cot, preferred_element_type=jnp.float32
        ).astype(jnp.bfloat16),
        "dp",
        scatter_dimension=0,
        tiled=True,
    )
    return (layer_out, input_grad, weight_grad, down_grad)


def over_z(rows, bit):
    return lax.ppermute(rows, "expert", [(i, i ^ bit) for i in range(lax.axis_size("expert"))])


def over_dp(rows, bit):
    return lax.ppermute(rows, "dp", [(i, i ^ bit) for i in range(lax.axis_size("dp"))])


def add(kept, other):
    return kept.astype(jnp.float32) + other.astype(jnp.float32)


def narrow(rows):
    return rows.astype(jnp.bfloat16)


def dot_last(a, b):
    return lax.dot_general(a, b, (((1,), (1,)), ((), ())), preferred_element_type=jnp.float32)


def dot_plain(a, b):
    return lax.dot_general(a, b, (((1,), (0,)), ((), ())), preferred_element_type=jnp.float32)


def dot_first(a, b):
    return lax.dot_general(a, b, (((0,), (0,)), ((), ())), preferred_element_type=jnp.float32)


UNIT_TILE = 256
WIDTH_TILE = 512


def place_rows(pieces, rows):
    start = 0
    for piece in pieces:
        count = piece.shape[0]
        rows[pl.ds(start, count), :] = piece[...]
        start += count


def forward_kernel(spread, collect, *refs):
    del collect
    pieces, refs = refs[:5], refs[5:]
    gate_a, gate_b, up_a, up_b, down_a, down_b, out, gate_out, up_out, mask, weighted, rows = refs
    step = pl.program_id(0)
    tiles = weighted.shape[1] // UNIT_TILE
    features = gate_a.shape[1]

    @pl.when(step == 0)
    def _():
        place_rows(pieces, rows)
        mask[...] = dot_plain(rows[:, features:], spread[...])

    def units(gate_w, up_w):
        token_rows = rows[:, :features]
        gate_pre = dot_last(token_rows, gate_w[...])
        up_pre = dot_last(token_rows, up_w[...])
        gate_out[...] = gate_pre
        up_out[...] = up_pre
        hidden = gate_pre * jax.nn.sigmoid(gate_pre) * up_pre
        at = pl.multiple_of(step * UNIT_TILE, UNIT_TILE)
        weighted[:, pl.ds(at, UNIT_TILE)] = (hidden * mask[...]).astype(jnp.bfloat16)

    @pl.when(step < tiles // 2)
    def _():
        units(gate_a, up_a)

    @pl.when((step >= tiles // 2) & (step < tiles))
    def _():
        units(gate_b, up_b)

    @pl.when(step >= tiles)
    def _():
        half = down_a.shape[0]
        total = dot_plain(weighted[:, :half], down_a[...]) + dot_plain(weighted[:, half:], down_b[...])
        out[...] = total.astype(jnp.bfloat16)


def backward_kernel(spread, collect, *refs):
    del spread
    pieces, refs = refs[:6], refs[6:]
    gate_a, gate_b, up_a, up_b, down_a, down_b, gate_in, up_in, mask, out, product_out, rows, gate_grad, up_grad, product = refs
    step = pl.program_id(0)
    tiles = gate_grad.shape[1] // UNIT_TILE

    @pl.when(step == 0)
    def _():
        place_rows(pieces, rows)
        product[...] = jnp.zeros_like(product)

    def units(down_w):
        hidden_grad = dot_last(rows[...], down_w[...])
        gate_pre, up_pre, weight = gate_in[...], up_in[...], mask[...]
        sig = jax.nn.sigmoid(gate_pre)
        gate_sig = gate_pre * sig
        product[...] += jnp.where(weight > 0, gate_sig * up_pre * hidden_grad, 0.0)
        hidden_grad = hidden_grad * weight
        at = pl.multiple_of(step * UNIT_TILE, UNIT_TILE)
        slope = sig * (1.0 + gate_pre * (1.0 - sig))
        gate_grad[:, pl.ds(at, UNIT_TILE)] = (hidden_grad * up_pre * slope).astype(jnp.bfloat16)
        up_grad[:, pl.ds(at, UNIT_TILE)] = (hidden_grad * gate_sig).astype(jnp.bfloat16)

    @pl.when(step < tiles // 2)
    def _():
        units(down_a)

    @pl.when((step >= tiles // 2) & (step < tiles))
    def _():
        units(down_b)

    @pl.when(step == tiles)
    def _():
        product_out[...] = dot_plain(product[...].astype(jnp.bfloat16), collect[...]).astype(jnp.bfloat16)

    @pl.when(step >= tiles)
    def _():
        half = gate_a.shape[0]
        total = dot_plain(gate_grad[:, :half], gate_a[...]) + dot_plain(gate_grad[:, half:], gate_b[...])
        total += dot_plain(up_grad[:, :half], up_a[...]) + dot_plain(up_grad[:, half:], up_b[...])
        out[...] = total.astype(jnp.bfloat16)


def merge_kernel(gate, up, down, merged):
    for slot, part in enumerate((gate, up, down)):
        merged[slot] = part[...].reshape(merged.shape[1:])


def merge_units(gate, up, down):
    units, experts, features = gate.shape
    tile = 32
    block = pl.BlockSpec((tile, experts, features), lambda i: (i, 0, 0))
    return pl.pallas_call(
        merge_kernel,
        grid=(units // tile,),
        in_specs=[block] * 3,
        out_specs=pl.BlockSpec((3, tile * experts, features), lambda i: (0, i, 0)),
        out_shape=jax.ShapeDtypeStruct((3, units * experts, features), gate.dtype),
        compiler_params=pltpu.CompilerParams(**PARAMS),
        cost_estimate=pl.CostEstimate(flops=0, bytes_accessed=12 * gate.size, transcendentals=0),
        name="merge_units",
    )(gate, up, down)


def whole(array):
    return pl.BlockSpec(array.shape, lambda i: (0, 0))


def by_units(array, slot, first):
    last = array.shape[1] // UNIT_TILE - 1
    return pl.BlockSpec((None, UNIT_TILE, array.shape[2]), lambda i: (slot, jnp.clip(i - first, 0, last), 0))


def by_width(array, slot, first):
    return pl.BlockSpec((None, array.shape[1], WIDTH_TILE), lambda i: (slot, 0, jnp.maximum(i - first, 0)))


def unit_columns(rows, tiles):
    return pl.BlockSpec((rows, UNIT_TILE), lambda i: (0, jnp.minimum(i, tiles - 1)))


def width_columns(rows, tiles):
    return pl.BlockSpec((rows, WIDTH_TILE), lambda i: (0, jnp.maximum(i - tiles, 0)))


def cost(rows, units, features, products):
    return pl.CostEstimate(
        flops=2 * rows * units * features * products,
        bytes_accessed=6 * units * features + 4 * rows * features,
        transcendentals=rows * units,
    )


PARAMS = dict(dimension_semantics=("arbitrary",), vmem_limit_bytes=24 * 1024 * 1024)


def forward(tables, pieces, weights):
    half, features = weights[0].shape[1:]
    rows = sum(piece.shape[0] for piece in pieces)
    tiles = 2 * half // UNIT_TILE
    operands = [*tables, *pieces, *weights * 3]
    specs = [whole(x) for x in (*tables, *pieces)]
    specs += [by_units(w, slot, n * tiles // 2) for slot in range(2) for n, w in enumerate(weights)]
    specs += [by_width(w, 2, tiles) for w in weights]
    return pl.pallas_call(
        forward_kernel,
        grid=(tiles + features // WIDTH_TILE,),
        in_specs=specs,
        out_specs=[
            width_columns(rows, tiles),
            unit_columns(rows, tiles),
            unit_columns(rows, tiles),
            pl.BlockSpec((rows, UNIT_TILE), lambda i: (0, 0)),
            pl.BlockSpec((rows, 2 * half), lambda i: (0, 0)),
        ],
        out_shape=[
            jax.ShapeDtypeStruct((rows, features), jnp.bfloat16),
            jax.ShapeDtypeStruct((rows, 2 * half), jnp.float32),
            jax.ShapeDtypeStruct((rows, 2 * half), jnp.float32),
            jax.ShapeDtypeStruct((rows, UNIT_TILE), jnp.float32),
            jax.ShapeDtypeStruct((rows, 2 * half), jnp.bfloat16),
        ],
        scratch_shapes=[pltpu.VMEM((rows, pieces[0].shape[1]), jnp.bfloat16)],
        compiler_params=pltpu.CompilerParams(**PARAMS),
        cost_estimate=cost(rows, 2 * half, features, 3),
        name="forward_products",
    )(*operands)


def backward(tables, pieces, weights, gate_pre, up_pre, mask):
    half, features = weights[0].shape[1:]
    rows = sum(piece.shape[0] for piece in pieces)
    tiles = 2 * half // UNIT_TILE
    operands = [*tables, *pieces, *weights * 3, gate_pre, up_pre, mask]
    specs = [whole(x) for x in (*tables, *pieces)]
    specs += [by_width(w, slot, tiles) for slot in range(2) for w in weights]
    specs += [by_units(w, 2, n * tiles // 2) for n, w in enumerate(weights)]
    specs += [unit_columns(rows, tiles), unit_columns(rows, tiles), whole(mask)]
    side = tables[1].shape[1]
    return pl.pallas_call(
        backward_kernel,
        grid=(tiles + features // WIDTH_TILE,),
        in_specs=specs,
        out_specs=[
            width_columns(rows, tiles),
            pl.BlockSpec((rows, side), lambda i: (0, 0)),
            pl.BlockSpec((rows, features), lambda i: (0, 0)),
        ],
        out_shape=[
            jax.ShapeDtypeStruct((rows, features), jnp.bfloat16),
            jax.ShapeDtypeStruct((rows, side), jnp.bfloat16),
            jax.ShapeDtypeStruct((rows, features), jnp.bfloat16),
        ],
        scratch_shapes=[
            pltpu.VMEM((rows, 2 * half), jnp.bfloat16),
            pltpu.VMEM((rows, 2 * half), jnp.bfloat16),
            pltpu.VMEM((rows, UNIT_TILE), jnp.float32),
        ],
        compiler_params=pltpu.CompilerParams(**PARAMS),
        cost_estimate=cost(rows, 2 * half, features, 3),
        name="backward_products",
    )(*operands)


def share_kernel(weighted, rows, other, out):
    total = dot_first(weighted[...], rows[...]) + other[...].astype(jnp.float32)
    out[...] = total.astype(jnp.bfloat16).reshape(out.shape)


def finish_share(weighted, rows, other, local_experts):
    count, features = rows.shape
    units = other.shape[0] // local_experts
    tile = UNIT_TILE // local_experts
    return pl.pallas_call(
        share_kernel,
        grid=(units // tile,),
        in_specs=[
            pl.BlockSpec((count, UNIT_TILE), lambda i: (0, i)),
            whole(rows),
            pl.BlockSpec((UNIT_TILE, features), lambda i: (i, 0)),
        ],
        out_specs=pl.BlockSpec((tile, local_experts, features), lambda i: (i, 0, 0)),
        out_shape=jax.ShapeDtypeStruct((units, local_experts, features), jnp.bfloat16),
        compiler_params=pltpu.CompilerParams(**PARAMS),
        cost_estimate=pl.CostEstimate(
            flops=2 * count * other.size, bytes_accessed=4 * other.size, transcendentals=0
        ),
        name="finish_share",
    )(weighted, rows, other)


def local_tokens(tokens, out_grad, expert_ids, slot_pos, combine_weight, w_gate, w_up, w_down):
    units, local_experts, width = w_gate.shape
    experts = local_experts * lax.axis_size("expert")
    first_expert = lax.axis_index("expert") * local_experts
    unit_rows = units * local_experts
    picked = (expert_ids[:, :, None] == jnp.arange(experts, dtype=jnp.int32)) & (slot_pos >= 0)[:, :, None]
    weight = jnp.sum(jnp.where(picked, combine_weight[:, :, None], 0.0), axis=1)
    high = lax.reduce_precision(weight, 8, 7)
    side = -(-2 * experts // 128) * 128
    routed = jnp.concatenate([high, weight - high], axis=1).astype(jnp.bfloat16)
    routed = jnp.pad(routed, ((0, 0), (0, side - 2 * experts)))
    unit_expert = first_expert + jnp.arange(UNIT_TILE, dtype=jnp.int32) % local_experts
    columns = jnp.arange(side, dtype=jnp.int32)
    spread = (columns[:, None] % experts == unit_expert[None, :]) & (columns < 2 * experts)[:, None]
    collect = (unit_expert[:, None] == columns[None, :]).astype(jnp.bfloat16)
    tables = (spread.astype(jnp.bfloat16), collect)

    own_t = jnp.concatenate([tokens, routed], axis=1)
    own_t, own_g, w_gate = lax.optimization_barrier((own_t, out_grad, w_gate))
    column_t = [over_z(own_t, bit) for bit in (2, 1, 3)]
    own_gx = over_dp(own_g, 2)
    weights = merge_units(w_gate, w_up, w_down)
    column_t, own_gx, own_g, weights = lax.optimization_barrier((column_t, own_gx, own_g, weights))

    pieces_t = [own_t, *column_t]
    column_tx = over_dp(jnp.concatenate(pieces_t, axis=0), 2)
    column_g = [over_z(own_g, bit) for bit in (2, 1, 3)]
    weights_b = over_dp(weights, 1)
    column_g, column_tx = lax.optimization_barrier((column_g, column_tx))

    away_gx = over_dp(jnp.concatenate(column_g, axis=0), 2)
    weights = [weights, weights_b]
    out_part, gate_pre, up_pre, mask, weighted = forward(tables, [*pieces_t, column_tx], weights)
    out_part, away_gx = lax.optimization_barrier((out_part, away_gx))

    half = out_part.shape[0] // 2
    pair, block = half // 2, half // 4
    out_x = over_dp(out_part[half:], 2)
    grad_pieces = [out_grad, *column_g, own_gx, away_gx]
    grad_part, product_part, grad_rows = backward(tables, grad_pieces, weights, gate_pre, up_pre, mask)
    weighted_b = weighted[:, unit_rows:]
    grad_part, product_part, out_x, weighted_b = lax.optimization_barrier((grad_part, product_part, out_x, weighted_b))

    grad_part = jnp.concatenate([grad_part, product_part], axis=1)
    near_x = over_dp(grad_part[half + pair :], 2)
    out_sum = add(out_part[:half], out_x)
    out_near = over_z(narrow(out_sum[pair:]), 1)
    share_b = narrow(dot_first(weighted_b, grad_rows))
    near_x, out_near, share_b = lax.optimization_barrier((near_x, out_near, share_b))

    grad_near = over_z(narrow(add(grad_part[pair:half], near_x)), 1)
    pair_x = over_dp(grad_part[half : half + pair], 2)
    out_sum = add(out_sum[:pair], out_near)
    out_far = over_z(narrow(out_sum[block:]), 2)
    other_share = over_dp(share_b, 1)
    grad_near, pair_x, out_far, other_share = lax.optimization_barrier((grad_near, pair_x, out_far, other_share))

    sums = add(add(grad_part[:pair], pair_x), grad_near)
    grad_far = over_z(narrow(sums[block:]), 2)
    layer_out = narrow(add(out_sum[:block], out_far))
    down_grad = finish_share(weighted, grad_rows, other_share, local_experts)
    grad_far, down_grad, layer_out = lax.optimization_barrier((grad_far, down_grad, layer_out))
    sums = add(sums[:block], grad_far)
    input_grad = narrow(sums[:, :width])
    per_expert = sums[:, width : width + experts]
    weight_grad = jnp.sum(jnp.where(picked, per_expert[:, None, :], 0.0), axis=2)
    return (layer_out, input_grad, weight_grad, down_grad)


def plan(tokens, out_grad, expert_ids, slot_pos, combine_weight, w_gate, w_up, w_down):
    args = (tokens, out_grad, expert_ids, slot_pos, combine_weight, w_gate, w_up, w_down)
    slots = tokens.shape[0] * expert_ids.shape[1] // lax.axis_size("expert")
    unit_rows = w_gate.shape[0] * w_gate.shape[1]
    tiled = w_gate.shape[0] % 64 == 0 and unit_rows % UNIT_TILE == 0 and UNIT_TILE % w_gate.shape[1] == 0
    tiled = tiled and w_gate.shape[2] % WIDTH_TILE == 0 and tokens.shape[0] % 32 == 0
    four = lax.axis_size("expert") == 4 and lax.axis_size("dp") == 4
    if tokens.shape[0] < slots and tiled and four:
        return local_tokens(*args)
    return local(*args)


def solution(mesh):
    in_specs = (
        P(("groups", "expert", "dp"), None),
        P(("groups", "expert", "dp"), None),
        P(("groups", "expert", "dp"), None),
        P(("groups", "expert", "dp"), None),
        P(("groups", "expert", "dp"), None),
        P("dp", "expert", None),
        P("dp", "expert", None),
        P("dp", "expert", None),
    )
    out_specs = (
        P(("groups", "expert", "dp"), None),
        P(("groups", "expert", "dp"), None),
        P(("groups", "expert", "dp"), None),
        P(("groups", "dp"), "expert", None),
    )
    return jax.shard_map(plan, mesh=mesh, in_specs=in_specs, out_specs=out_specs, check_vma=False)
```

```python
import jax
import jax.numpy as jnp
from jax import lax
from jax.experimental import pallas as pl
from jax.experimental.pallas import tpu as pltpu
from jax.sharding import PartitionSpec as P


def slot_places(expert_ids, slot_pos, local_experts, row_total, capacity):
    flat_place = (
        expert_ids % local_experts * row_total + expert_ids // local_experts * capacity + slot_pos
    )
    return jnp.where(slot_pos >= 0, flat_place, -1)


def local(tokens, out_grad, expert_ids, slot_pos, combine_weight, w_gate, w_up, w_down):
    local_experts = w_gate.shape[1]
    expert_peers = lax.axis_size("expert")
    tok_count = tokens.shape[0]
    top_count = expert_ids.shape[1]
    model_width = tokens.shape[1]
    capacity = tok_count * top_count // (local_experts * expert_peers)
    row_total = expert_peers * capacity
    slot_count = local_experts * row_total
    kept_mask = slot_pos >= 0
    flat_place = slot_places(expert_ids, slot_pos, local_experts, row_total, capacity)
    places = jnp.arange(slot_count, dtype=jnp.int32)
    onehot = (flat_place[:, :, None] == places[None, None, :]).astype(jnp.float32)
    present = jnp.sum(onehot, axis=1)
    weighted = jnp.sum(onehot * combine_weight[:, :, None], axis=1)
    sent_rows = jnp.einsum(
        "tw,td->wd", present.astype(jnp.bfloat16), tokens, preferred_element_type=jnp.float32
    )
    sent_cot = jnp.einsum(
        "tw,td->wd", weighted, out_grad.astype(jnp.float32), precision=lax.Precision.HIGHEST
    )
    sent_rows = sent_rows.astype(jnp.bfloat16).reshape(local_experts, row_total, model_width)
    sent_cot = sent_cot.astype(jnp.bfloat16).reshape(local_experts, row_total, model_width)
    expert_rows, expert_cot = (
        lax.all_to_all(sent_rows, "expert", split_axis=1, concat_axis=1, tiled=True),
        lax.all_to_all(sent_cot, "expert", split_axis=1, concat_axis=1, tiled=True),
    )
    gate_piece = lax.all_gather(w_gate, "dp", axis=0, tiled=True)
    up_piece = lax.all_gather(w_up, "dp", axis=0, tiled=True)
    down_piece = lax.all_gather(w_down, "dp", axis=0, tiled=True)
    gate_pre = jnp.einsum(
        "nld,lrd->lnr", gate_piece, expert_rows, preferred_element_type=jnp.float32
    )
    up_pre = jnp.einsum("nld,lrd->lnr", up_piece, expert_rows, preferred_element_type=jnp.float32)
    sigmoid_val = jax.nn.sigmoid(gate_pre)
    hidden = (gate_pre * sigmoid_val * up_pre).astype(jnp.bfloat16)
    expert_out = jnp.einsum("lnr,nld->lrd", hidden, down_piece, preferred_element_type=jnp.float32)
    hidden_grad = jnp.einsum(
        "nld,lrd->lnr", down_piece, expert_cot, preferred_element_type=jnp.float32
    )
    gate_grad = (
        hidden_grad * up_pre * sigmoid_val * (1.0 + gate_pre * (1.0 - sigmoid_val))
    ).astype(jnp.bfloat16)
    up_grad = (hidden_grad * gate_pre * sigmoid_val).astype(jnp.bfloat16)
    slot_back = jnp.einsum(
        "lnr,nld->lrd", gate_grad, gate_piece, preferred_element_type=jnp.float32
    )
    slot_back = slot_back + jnp.einsum(
        "lnr,nld->lrd", up_grad, up_piece, preferred_element_type=jnp.float32
    )
    hidden_all, expert_out, slot_back = (hidden, expert_out, slot_back)
    back_out, back_grad = (
        lax.all_to_all(
            expert_out.astype(jnp.bfloat16), "expert", split_axis=1, concat_axis=1, tiled=True
        ),
        lax.all_to_all(
            slot_back.astype(jnp.bfloat16), "expert", split_axis=1, concat_axis=1, tiled=True
        ),
    )
    back_out = back_out.reshape(slot_count, model_width)
    back_grad = back_grad.reshape(slot_count, model_width)
    safe_place = jnp.maximum(flat_place, 0)
    picked_out = jnp.where(
        kept_mask[:, :, None], jnp.take(back_out, safe_place, axis=0).astype(jnp.float32), 0.0
    )
    picked_grad = jnp.where(
        kept_mask[:, :, None], jnp.take(back_grad, safe_place, axis=0).astype(jnp.float32), 0.0
    )
    layer_out = jnp.sum(combine_weight[:, :, None] * picked_out, axis=1).astype(jnp.bfloat16)
    input_grad = jnp.sum(picked_grad, axis=1).astype(jnp.bfloat16)
    weight_grad = jnp.sum(picked_out * out_grad.astype(jnp.float32)[:, None, :], axis=2)
    down_grad = lax.psum_scatter(
        jnp.einsum(
            "lnr,lrd->nld", hidden_all, expert_cot, preferred_element_type=jnp.float32
        ).astype(jnp.bfloat16),
        "dp",
        scatter_dimension=0,
        tiled=True,
    )
    return (layer_out, input_grad, weight_grad, down_grad)


def over_z(rows, bit):
    return lax.ppermute(rows, "expert", [(i, i ^ bit) for i in range(lax.axis_size("expert"))])


def over_dp(rows, bit):
    return lax.ppermute(rows, "dp", [(i, i ^ bit) for i in range(lax.axis_size("dp"))])


def add(kept, other):
    return kept.astype(jnp.float32) + other.astype(jnp.float32)


def narrow(rows):
    return rows.astype(jnp.bfloat16)


def dot_last(a, b):
    return lax.dot_general(a, b, (((1,), (1,)), ((), ())), preferred_element_type=jnp.float32)


def dot_plain(a, b):
    return lax.dot_general(a, b, (((1,), (0,)), ((), ())), preferred_element_type=jnp.float32)


def dot_first(a, b):
    return lax.dot_general(a, b, (((0,), (0,)), ((), ())), preferred_element_type=jnp.float32)


UNIT_TILE = 256
WIDTH_TILE = 512


def place_rows(pieces, rows):
    start = 0
    for piece in pieces:
        count = piece.shape[0]
        rows[pl.ds(start, count), :] = piece[...]
        start += count


def bring(sources, held, sems, order):
    copies = {}
    for half, slot in order:
        copy = pltpu.make_async_copy(sources[half].at[slot], held[half].at[slot], sems.at[half, slot])
        copy.start()
        copies[half, slot] = copy
    return copies


def unit_tiles(half_rows):
    return [(half, at) for half in range(2) for at in range(0, half_rows, UNIT_TILE)]


def forward_kernel(spread, *refs):
    pieces, (weights_a, weights_b, out, gate_out, up_out, mask, weighted, rows, held_a, held_b, sems) = refs[:5], refs[5:]
    held = (held_a, held_b)
    order = [(0, 0), (0, 1), (1, 0), (1, 1), (0, 2), (1, 2)]
    copies = bring((weights_a, weights_b), held, sems, order)
    half_rows, features = held_a.shape[1:]
    place_rows(pieces, rows)
    mask[...] = dot_plain(rows[:, features:], spread[...])
    for half, at in unit_tiles(half_rows):
        if at == 0:
            copies[half, 0].wait()
            copies[half, 1].wait()
        units = pl.ds(at, UNIT_TILE)
        gate_pre = dot_last(rows[:, :features], held[half][0, units, :])
        up_pre = dot_last(rows[:, :features], held[half][1, units, :])
        columns = pl.ds(half * half_rows + at, UNIT_TILE)
        gate_out[:, columns] = gate_pre
        up_out[:, columns] = up_pre
        hidden = gate_pre * jax.nn.sigmoid(gate_pre) * up_pre
        weighted[:, columns] = (hidden * mask[...]).astype(jnp.bfloat16)
    copies[0, 2].wait()
    copies[1, 2].wait()
    for at in range(0, features, WIDTH_TILE):
        columns = pl.ds(at, WIDTH_TILE)
        total = dot_plain(weighted[:, :half_rows], held_a[2, :, columns])
        total += dot_plain(weighted[:, half_rows:], held_b[2, :, columns])
        out[:, columns] = total.astype(jnp.bfloat16)


def backward_kernel(collect, *refs):
    pieces, refs = refs[:6], refs[6:]
    weights_a, weights_b, gate_in, up_in, mask, out, product_out, rows, gate_grad, up_grad, product, held_a, held_b, sems = refs
    held = (held_a, held_b)
    order = [(0, 2), (1, 2), (0, 0), (1, 0), (0, 1), (1, 1)]
    copies = bring((weights_a, weights_b), held, sems, order)
    half_rows, features = held_a.shape[1:]
    place_rows(pieces, rows)
    for half, at in unit_tiles(half_rows):
        if at == 0:
            copies[half, 2].wait()
        hidden_grad = dot_last(rows[...], held[half][2, pl.ds(at, UNIT_TILE), :])
        columns = pl.ds(half * half_rows + at, UNIT_TILE)
        gate_pre, up_pre, weight = gate_in[:, columns], up_in[:, columns], mask[...]
        sig = jax.nn.sigmoid(gate_pre)
        gate_sig = gate_pre * sig
        term = jnp.where(weight > 0, gate_sig * up_pre * hidden_grad, 0.0)
        product[...] = term if half == 0 and at == 0 else product[...] + term
        hidden_grad = hidden_grad * weight
        slope = sig * (1.0 + gate_pre * (1.0 - sig))
        gate_grad[:, columns] = (hidden_grad * up_pre * slope).astype(jnp.bfloat16)
        up_grad[:, columns] = (hidden_grad * gate_sig).astype(jnp.bfloat16)
    product_out[...] = dot_plain(product[...].astype(jnp.bfloat16), collect[...]).astype(jnp.bfloat16)
    for half, slot in order[2:]:
        copies[half, slot].wait()
    for at in range(0, features, WIDTH_TILE):
        columns = pl.ds(at, WIDTH_TILE)
        total = dot_plain(gate_grad[:, :half_rows], held_a[0, :, columns])
        total += dot_plain(gate_grad[:, half_rows:], held_b[0, :, columns])
        total += dot_plain(up_grad[:, :half_rows], held_a[1, :, columns])
        total += dot_plain(up_grad[:, half_rows:], held_b[1, :, columns])
        out[:, columns] = total.astype(jnp.bfloat16)


def merge_kernel(gate, up, down, merged):
    for slot, part in enumerate((gate, up, down)):
        merged[slot] = part[...].reshape(merged.shape[1:])


def merge_units(gate, up, down):
    units, experts, features = gate.shape
    tile = 32
    block = pl.BlockSpec((tile, experts, features), lambda i: (i, 0, 0))
    return pl.pallas_call(
        merge_kernel,
        grid=(units // tile,),
        in_specs=[block] * 3,
        out_specs=pl.BlockSpec((3, tile * experts, features), lambda i: (0, i, 0)),
        out_shape=jax.ShapeDtypeStruct((3, units * experts, features), gate.dtype),
        compiler_params=pltpu.CompilerParams(**PARAMS),
        cost_estimate=pl.CostEstimate(flops=0, bytes_accessed=12 * gate.size, transcendentals=0),
        name="merge_units",
    )(gate, up, down)


def whole(array):
    return pl.BlockSpec(array.shape, lambda i: (0, 0))


def cost(rows, units, features, products):
    return pl.CostEstimate(
        flops=2 * rows * units * features * products,
        bytes_accessed=6 * units * features + 4 * rows * features,
        transcendentals=rows * units,
    )


PARAMS = dict(dimension_semantics=("arbitrary",), vmem_limit_bytes=24 * 1024 * 1024)
IN_VMEM = pl.BlockSpec(memory_space=pltpu.VMEM)


def products(kernel, name, table, pieces, weights, saved, out_shape, scratch):
    half, features = weights[0].shape[1:]
    rows = sum(piece.shape[0] for piece in pieces)
    held = [pltpu.VMEM(w.shape, w.dtype) for w in weights]
    return pl.pallas_call(
        kernel,
        in_specs=[IN_VMEM] * (1 + len(pieces)) + [pl.BlockSpec(memory_space=pl.ANY)] * 2 + [IN_VMEM] * len(saved),
        out_specs=[IN_VMEM] * len(out_shape),
        out_shape=out_shape,
        scratch_shapes=[*scratch, *held, pltpu.SemaphoreType.DMA((2, 3))],
        compiler_params=pltpu.CompilerParams(vmem_limit_bytes=PRODUCT_VMEM),
        cost_estimate=cost(rows, 2 * half, features, 3),
        name=name,
    )(table, *pieces, *weights, *saved)


PRODUCT_VMEM = 34 * 1024 * 1024


def forward(spread, pieces, weights):
    half, features = weights[0].shape[1:]
    rows = sum(piece.shape[0] for piece in pieces)
    shape = jax.ShapeDtypeStruct
    out_shape = [
        shape((rows, features), jnp.bfloat16),
        shape((rows, 2 * half), jnp.float32),
        shape((rows, 2 * half), jnp.float32),
        shape((rows, UNIT_TILE), jnp.float32),
        shape((rows, 2 * half), jnp.bfloat16),
    ]
    scratch = [pltpu.VMEM((rows, pieces[0].shape[1]), jnp.bfloat16)]
    return products(forward_kernel, "forward_products", spread, pieces, weights, [], out_shape, scratch)


def backward(collect, pieces, weights, gate_pre, up_pre, mask):
    half, features = weights[0].shape[1:]
    rows = sum(piece.shape[0] for piece in pieces)
    shape = jax.ShapeDtypeStruct
    out_shape = [
        shape((rows, features), jnp.bfloat16),
        shape((rows, collect.shape[1]), jnp.bfloat16),
        shape((rows, features), jnp.bfloat16),
    ]
    scratch = [pltpu.VMEM((rows, 2 * half), jnp.bfloat16)] * 2 + [pltpu.VMEM((rows, UNIT_TILE), jnp.float32)]
    saved = [gate_pre, up_pre, mask]
    return products(backward_kernel, "backward_products", collect, pieces, weights, saved, out_shape, scratch)


def share_kernel(weighted, rows, other, out):
    total = dot_first(weighted[...], rows[...]) + other[...].astype(jnp.float32)
    out[...] = total.astype(jnp.bfloat16).reshape(out.shape)


def finish_share(weighted, rows, other, local_experts):
    count, features = rows.shape
    units = other.shape[0] // local_experts
    tile = UNIT_TILE // local_experts
    return pl.pallas_call(
        share_kernel,
        grid=(units // tile,),
        in_specs=[
            pl.BlockSpec((count, UNIT_TILE), lambda i: (0, i)),
            whole(rows),
            pl.BlockSpec((UNIT_TILE, features), lambda i: (i, 0)),
        ],
        out_specs=pl.BlockSpec((tile, local_experts, features), lambda i: (i, 0, 0)),
        out_shape=jax.ShapeDtypeStruct((units, local_experts, features), jnp.bfloat16),
        compiler_params=pltpu.CompilerParams(**PARAMS),
        cost_estimate=pl.CostEstimate(
            flops=2 * count * other.size, bytes_accessed=4 * other.size, transcendentals=0
        ),
        name="finish_share",
    )(weighted, rows, other)


def local_tokens(tokens, out_grad, expert_ids, slot_pos, combine_weight, w_gate, w_up, w_down):
    units, local_experts, width = w_gate.shape
    experts = local_experts * lax.axis_size("expert")
    first_expert = lax.axis_index("expert") * local_experts
    unit_rows = units * local_experts
    picked = (expert_ids[:, :, None] == jnp.arange(experts, dtype=jnp.int32)) & (slot_pos >= 0)[:, :, None]
    weight = jnp.sum(jnp.where(picked, combine_weight[:, :, None], 0.0), axis=1)
    high = lax.reduce_precision(weight, 8, 7)
    side = -(-2 * experts // 128) * 128
    routed = jnp.concatenate([high, weight - high], axis=1).astype(jnp.bfloat16)
    routed = jnp.pad(routed, ((0, 0), (0, side - 2 * experts)))
    unit_expert = first_expert + jnp.arange(UNIT_TILE, dtype=jnp.int32) % local_experts
    columns = jnp.arange(side, dtype=jnp.int32)
    spread = (columns[:, None] % experts == unit_expert[None, :]) & (columns < 2 * experts)[:, None]
    collect = (unit_expert[:, None] == columns[None, :]).astype(jnp.bfloat16)
    spread = spread.astype(jnp.bfloat16)

    own_t = jnp.concatenate([tokens, routed], axis=1)
    own_t, own_g, w_gate = lax.optimization_barrier((own_t, out_grad, w_gate))
    column_t = [over_z(own_t, bit) for bit in (2, 1, 3)]
    own_gx = over_dp(own_g, 2)
    weights = merge_units(w_gate, w_up, w_down)
    column_t, own_gx, own_g, weights = lax.optimization_barrier((column_t, own_gx, own_g, weights))

    pieces_t = [own_t, *column_t]
    column_tx = over_dp(jnp.concatenate(pieces_t, axis=0), 2)
    column_g = [over_z(own_g, bit) for bit in (2, 1, 3)]
    weights_b = over_dp(weights, 1)
    column_g, column_tx = lax.optimization_barrier((column_g, column_tx))

    away_gx = over_dp(jnp.concatenate(column_g, axis=0), 2)
    weights = [weights, weights_b]
    out_part, gate_pre, up_pre, mask, weighted = forward(spread, [*pieces_t, column_tx], weights)
    out_part, away_gx = lax.optimization_barrier((out_part, away_gx))

    half = out_part.shape[0] // 2
    pair, block = half // 2, half // 4
    out_x = over_dp(out_part[half:], 2)
    grad_pieces = [out_grad, *column_g, own_gx, away_gx]
    grad_part, product_part, grad_rows = backward(collect, grad_pieces, weights, gate_pre, up_pre, mask)
    weighted_b = weighted[:, unit_rows:]
    grad_part, product_part, out_x, weighted_b = lax.optimization_barrier((grad_part, product_part, out_x, weighted_b))

    grad_part = jnp.concatenate([grad_part, product_part], axis=1)
    near_x = over_dp(grad_part[half + pair :], 2)
    out_sum = add(out_part[:half], out_x)
    out_near = over_z(narrow(out_sum[pair:]), 1)
    share_b = narrow(dot_first(weighted_b, grad_rows))
    near_x, out_near, share_b = lax.optimization_barrier((near_x, out_near, share_b))

    grad_near = over_z(narrow(add(grad_part[pair:half], near_x)), 1)
    pair_x = over_dp(grad_part[half : half + pair], 2)
    out_sum = add(out_sum[:pair], out_near)
    out_far = over_z(narrow(out_sum[block:]), 2)
    other_share = over_dp(share_b, 1)
    grad_near, pair_x, out_far, other_share = lax.optimization_barrier((grad_near, pair_x, out_far, other_share))

    sums = add(add(grad_part[:pair], pair_x), grad_near)
    grad_far = over_z(narrow(sums[block:]), 2)
    layer_out = narrow(add(out_sum[:block], out_far))
    down_grad = finish_share(weighted, grad_rows, other_share, local_experts)
    grad_far, down_grad, layer_out = lax.optimization_barrier((grad_far, down_grad, layer_out))
    sums = add(sums[:block], grad_far)
    input_grad = narrow(sums[:, :width])
    per_expert = sums[:, width : width + experts]
    weight_grad = jnp.sum(jnp.where(picked, per_expert[:, None, :], 0.0), axis=2)
    return (layer_out, input_grad, weight_grad, down_grad)


def plan(tokens, out_grad, expert_ids, slot_pos, combine_weight, w_gate, w_up, w_down):
    args = (tokens, out_grad, expert_ids, slot_pos, combine_weight, w_gate, w_up, w_down)
    slots = tokens.shape[0] * expert_ids.shape[1] // lax.axis_size("expert")
    unit_rows = w_gate.shape[0] * w_gate.shape[1]
    tiled = w_gate.shape[0] % 64 == 0 and unit_rows % UNIT_TILE == 0 and UNIT_TILE % w_gate.shape[1] == 0
    tiled = tiled and w_gate.shape[2] % WIDTH_TILE == 0 and tokens.shape[0] % 32 == 0
    four = lax.axis_size("expert") == 4 and lax.axis_size("dp") == 4
    if tokens.shape[0] < slots and tiled and four:
        return local_tokens(*args)
    return local(*args)


def solution(mesh):
    in_specs = (
        P(("groups", "expert", "dp"), None),
        P(("groups", "expert", "dp"), None),
        P(("groups", "expert", "dp"), None),
        P(("groups", "expert", "dp"), None),
        P(("groups", "expert", "dp"), None),
        P("dp", "expert", None),
        P("dp", "expert", None),
        P("dp", "expert", None),
    )
    out_specs = (
        P(("groups", "expert", "dp"), None),
        P(("groups", "expert", "dp"), None),
        P(("groups", "expert", "dp"), None),
        P(("groups", "dp"), "expert", None),
    )
    return jax.shard_map(plan, mesh=mesh, in_specs=in_specs, out_specs=out_specs, check_vma=False)
```

```python
import functools

import jax
import jax.numpy as jnp
from jax import lax
from jax.experimental import pallas as pl
from jax.experimental.pallas import tpu as pltpu
from jax.sharding import PartitionSpec as P


def slot_places(expert_ids, slot_pos, local_experts, row_total, capacity):
    flat_place = (
        expert_ids % local_experts * row_total + expert_ids // local_experts * capacity + slot_pos
    )
    return jnp.where(slot_pos >= 0, flat_place, -1)


def local(tokens, out_grad, expert_ids, slot_pos, combine_weight, w_gate, w_up, w_down):
    local_experts = w_gate.shape[1]
    expert_peers = lax.axis_size("expert")
    tok_count = tokens.shape[0]
    top_count = expert_ids.shape[1]
    model_width = tokens.shape[1]
    capacity = tok_count * top_count // (local_experts * expert_peers)
    row_total = expert_peers * capacity
    slot_count = local_experts * row_total
    kept_mask = slot_pos >= 0
    flat_place = slot_places(expert_ids, slot_pos, local_experts, row_total, capacity)
    places = jnp.arange(slot_count, dtype=jnp.int32)
    onehot = (flat_place[:, :, None] == places[None, None, :]).astype(jnp.float32)
    present = jnp.sum(onehot, axis=1)
    weighted = jnp.sum(onehot * combine_weight[:, :, None], axis=1)
    sent_rows = jnp.einsum(
        "tw,td->wd", present.astype(jnp.bfloat16), tokens, preferred_element_type=jnp.float32
    )
    sent_cot = jnp.einsum(
        "tw,td->wd", weighted, out_grad.astype(jnp.float32), precision=lax.Precision.HIGHEST
    )
    sent_rows = sent_rows.astype(jnp.bfloat16).reshape(local_experts, row_total, model_width)
    sent_cot = sent_cot.astype(jnp.bfloat16).reshape(local_experts, row_total, model_width)
    expert_rows, expert_cot = (
        lax.all_to_all(sent_rows, "expert", split_axis=1, concat_axis=1, tiled=True),
        lax.all_to_all(sent_cot, "expert", split_axis=1, concat_axis=1, tiled=True),
    )
    gate_piece = lax.all_gather(w_gate, "dp", axis=0, tiled=True)
    up_piece = lax.all_gather(w_up, "dp", axis=0, tiled=True)
    down_piece = lax.all_gather(w_down, "dp", axis=0, tiled=True)
    gate_pre = jnp.einsum(
        "nld,lrd->lnr", gate_piece, expert_rows, preferred_element_type=jnp.float32
    )
    up_pre = jnp.einsum("nld,lrd->lnr", up_piece, expert_rows, preferred_element_type=jnp.float32)
    sigmoid_val = jax.nn.sigmoid(gate_pre)
    hidden = (gate_pre * sigmoid_val * up_pre).astype(jnp.bfloat16)
    expert_out = jnp.einsum("lnr,nld->lrd", hidden, down_piece, preferred_element_type=jnp.float32)
    hidden_grad = jnp.einsum(
        "nld,lrd->lnr", down_piece, expert_cot, preferred_element_type=jnp.float32
    )
    gate_grad = (
        hidden_grad * up_pre * sigmoid_val * (1.0 + gate_pre * (1.0 - sigmoid_val))
    ).astype(jnp.bfloat16)
    up_grad = (hidden_grad * gate_pre * sigmoid_val).astype(jnp.bfloat16)
    slot_back = jnp.einsum(
        "lnr,nld->lrd", gate_grad, gate_piece, preferred_element_type=jnp.float32
    )
    slot_back = slot_back + jnp.einsum(
        "lnr,nld->lrd", up_grad, up_piece, preferred_element_type=jnp.float32
    )
    hidden_all, expert_out, slot_back = (hidden, expert_out, slot_back)
    back_out, back_grad = (
        lax.all_to_all(
            expert_out.astype(jnp.bfloat16), "expert", split_axis=1, concat_axis=1, tiled=True
        ),
        lax.all_to_all(
            slot_back.astype(jnp.bfloat16), "expert", split_axis=1, concat_axis=1, tiled=True
        ),
    )
    back_out = back_out.reshape(slot_count, model_width)
    back_grad = back_grad.reshape(slot_count, model_width)
    safe_place = jnp.maximum(flat_place, 0)
    picked_out = jnp.where(
        kept_mask[:, :, None], jnp.take(back_out, safe_place, axis=0).astype(jnp.float32), 0.0
    )
    picked_grad = jnp.where(
        kept_mask[:, :, None], jnp.take(back_grad, safe_place, axis=0).astype(jnp.float32), 0.0
    )
    layer_out = jnp.sum(combine_weight[:, :, None] * picked_out, axis=1).astype(jnp.bfloat16)
    input_grad = jnp.sum(picked_grad, axis=1).astype(jnp.bfloat16)
    weight_grad = jnp.sum(picked_out * out_grad.astype(jnp.float32)[:, None, :], axis=2)
    down_grad = lax.psum_scatter(
        jnp.einsum(
            "lnr,lrd->nld", hidden_all, expert_cot, preferred_element_type=jnp.float32
        ).astype(jnp.bfloat16),
        "dp",
        scatter_dimension=0,
        tiled=True,
    )
    return (layer_out, input_grad, weight_grad, down_grad)


def over_z(rows, bit):
    return lax.ppermute(rows, "expert", [(i, i ^ bit) for i in range(lax.axis_size("expert"))])


def over_dp(rows, bit):
    return lax.ppermute(rows, "dp", [(i, i ^ bit) for i in range(lax.axis_size("dp"))])


def add(kept, other):
    return kept.astype(jnp.float32) + other.astype(jnp.float32)


def narrow(rows):
    return rows.astype(jnp.bfloat16)


def dot_last(a, b):
    return lax.dot_general(a, b, (((1,), (1,)), ((), ())), preferred_element_type=jnp.float32)


def dot_plain(a, b):
    return lax.dot_general(a, b, (((1,), (0,)), ((), ())), preferred_element_type=jnp.float32)


def dot_first(a, b):
    return lax.dot_general(a, b, (((0,), (0,)), ((), ())), preferred_element_type=jnp.float32)


UNIT_TILE = 256
WIDTH_TILE = 512


def place_rows(pieces, rows):
    start = 0
    for piece in pieces:
        count = piece.shape[0]
        rows[pl.ds(start, count), :] = piece[...]
        start += count


def payload_kernel(experts, tokens, ids, pos, weights, out):
    picks, count = ids.shape
    expert = lax.broadcasted_iota(jnp.int32, (experts, count), 0)
    weight = jnp.zeros((experts, count), jnp.float32)
    for k in range(picks):
        row = pl.ds(k, 1)
        weight += jnp.where((ids[row, :] == expert) & (pos[row, :] >= 0), weights[row, :], 0.0)
    high = weight.astype(jnp.bfloat16)
    low = (weight - high.astype(jnp.float32)).astype(jnp.bfloat16)
    both = jnp.concatenate([high, low], axis=0)
    width = tokens.shape[1]
    spot = (both.shape[0], out.shape[1] - width)
    same = lax.broadcasted_iota(jnp.int32, spot, 0) == lax.broadcasted_iota(jnp.int32, spot, 1)
    routed = dot_first(both, same.astype(jnp.float32).astype(jnp.bfloat16))
    out[:, :width] = tokens[...]
    out[:, width:] = routed.astype(jnp.bfloat16)


def payload(tokens, ids, pos, weights, experts, side):
    rows, width = tokens.shape
    return pl.pallas_call(
        functools.partial(payload_kernel, experts),
        in_specs=[IN_VMEM] * 4,
        out_specs=IN_VMEM,
        out_shape=jax.ShapeDtypeStruct((rows, width + side), tokens.dtype),
        name="payload",
    )(tokens, ids.T, pos.T, weights.T)


def bring(sources, held, sems, order):
    copies = {}
    for half, slot in order:
        copy = pltpu.make_async_copy(sources[half].at[slot], held[half].at[slot], sems.at[half, slot])
        copy.start()
        copies[half, slot] = copy
    return copies


def unit_tiles(half_rows):
    return [(half, at) for half in range(2) for at in range(0, half_rows, UNIT_TILE)]


def forward_kernel(spread, *refs):
    pieces, (weights_a, weights_b, out, gate_out, up_out, mask, weighted, rows, held_a, held_b, sems) = refs[:5], refs[5:]
    held = (held_a, held_b)
    order = [(0, 0), (0, 1), (1, 0), (1, 1), (0, 2), (1, 2)]
    copies = bring((weights_a, weights_b), held, sems, order)
    half_rows, features = held_a.shape[1:]
    place_rows(pieces, rows)
    mask[...] = dot_plain(rows[:, features:], spread[...])
    for half, at in unit_tiles(half_rows):
        if at == 0:
            copies[half, 0].wait()
            copies[half, 1].wait()
        units = pl.ds(at, UNIT_TILE)
        gate_pre = dot_last(rows[:, :features], held[half][0, units, :])
        up_pre = dot_last(rows[:, :features], held[half][1, units, :])
        columns = pl.ds(half * half_rows + at, UNIT_TILE)
        gate_out[:, columns] = gate_pre
        up_out[:, columns] = up_pre
        hidden = gate_pre * jax.nn.sigmoid(gate_pre) * up_pre
        weighted[:, columns] = (hidden * mask[...]).astype(jnp.bfloat16)
    copies[0, 2].wait()
    copies[1, 2].wait()
    for at in range(0, features, WIDTH_TILE):
        columns = pl.ds(at, WIDTH_TILE)
        total = dot_plain(weighted[:, :half_rows], held_a[2, :, columns])
        total += dot_plain(weighted[:, half_rows:], held_b[2, :, columns])
        out[:, columns] = total.astype(jnp.bfloat16)


def backward_kernel(collect, *refs):
    pieces, refs = refs[:6], refs[6:]
    weights_a, weights_b, gate_in, up_in, mask, weighted, out, product_out, rows, share, gate_grad, up_grad, product, held_a, held_b, sems = refs
    held = (held_a, held_b)
    order = [(0, 2), (1, 2), (0, 0), (1, 0), (0, 1), (1, 1)]
    copies = bring((weights_a, weights_b), held, sems, order)
    half_rows, features = held_a.shape[1:]
    place_rows(pieces, rows)
    for half, at in unit_tiles(half_rows):
        if at == 0:
            copies[half, 2].wait()
        hidden_grad = dot_last(rows[...], held[half][2, pl.ds(at, UNIT_TILE), :])
        columns = pl.ds(half * half_rows + at, UNIT_TILE)
        gate_pre, up_pre, weight = gate_in[:, columns], up_in[:, columns], mask[...]
        sig = jax.nn.sigmoid(gate_pre)
        gate_sig = gate_pre * sig
        term = jnp.where(weight > 0, gate_sig * up_pre * hidden_grad, 0.0)
        product[...] = term if half == 0 and at == 0 else product[...] + term
        hidden_grad = hidden_grad * weight
        slope = sig * (1.0 + gate_pre * (1.0 - sig))
        gate_grad[:, columns] = (hidden_grad * up_pre * slope).astype(jnp.bfloat16)
        up_grad[:, columns] = (hidden_grad * gate_sig).astype(jnp.bfloat16)
    product_out[...] = dot_plain(product[...].astype(jnp.bfloat16), collect[...]).astype(jnp.bfloat16)
    for at in range(0, half_rows, UNIT_TILE):
        part = dot_first(weighted[:, pl.ds(half_rows + at, UNIT_TILE)], rows[...])
        share[pl.ds(at, UNIT_TILE), :] = part.astype(jnp.bfloat16)
    for half, slot in order[2:]:
        copies[half, slot].wait()
    for at in range(0, features, WIDTH_TILE):
        columns = pl.ds(at, WIDTH_TILE)
        total = dot_plain(gate_grad[:, :half_rows], held_a[0, :, columns])
        total += dot_plain(gate_grad[:, half_rows:], held_b[0, :, columns])
        total += dot_plain(up_grad[:, :half_rows], held_a[1, :, columns])
        total += dot_plain(up_grad[:, half_rows:], held_b[1, :, columns])
        out[:, columns] = total.astype(jnp.bfloat16)


def merge_kernel(gate, up, down, merged):
    for slot, part in enumerate((gate, up, down)):
        merged[slot] = part[...].reshape(merged.shape[1:])


def merge_units(gate, up, down):
    units, experts, features = gate.shape
    tile = 32
    block = pl.BlockSpec((tile, experts, features), lambda i: (i, 0, 0))
    return pl.pallas_call(
        merge_kernel,
        grid=(units // tile,),
        in_specs=[block] * 3,
        out_specs=pl.BlockSpec((3, tile * experts, features), lambda i: (0, i, 0)),
        out_shape=jax.ShapeDtypeStruct((3, units * experts, features), gate.dtype),
        compiler_params=pltpu.CompilerParams(**PARAMS),
        cost_estimate=pl.CostEstimate(flops=0, bytes_accessed=12 * gate.size, transcendentals=0),
        name="merge_units",
    )(gate, up, down)


def whole(array):
    return pl.BlockSpec(array.shape, lambda i: (0, 0))


def cost(rows, units, features, products):
    return pl.CostEstimate(
        flops=2 * rows * units * features * products,
        bytes_accessed=6 * units * features + 4 * rows * features,
        transcendentals=rows * units,
    )


PARAMS = dict(dimension_semantics=("arbitrary",), vmem_limit_bytes=24 * 1024 * 1024)
IN_VMEM = pl.BlockSpec(memory_space=pltpu.VMEM)


def products(kernel, name, table, pieces, weights, saved, out_shape, scratch):
    half, features = weights[0].shape[1:]
    rows = sum(piece.shape[0] for piece in pieces)
    held = [pltpu.VMEM(w.shape, w.dtype) for w in weights]
    return pl.pallas_call(
        kernel,
        in_specs=[IN_VMEM] * (1 + len(pieces)) + [pl.BlockSpec(memory_space=pl.ANY)] * 2 + [IN_VMEM] * len(saved),
        out_specs=[IN_VMEM] * len(out_shape),
        out_shape=out_shape,
        scratch_shapes=[*scratch, *held, pltpu.SemaphoreType.DMA((2, 3))],
        compiler_params=pltpu.CompilerParams(vmem_limit_bytes=PRODUCT_VMEM),
        cost_estimate=cost(rows, 2 * half, features, 3),
        name=name,
    )(table, *pieces, *weights, *saved)


PRODUCT_VMEM = 34 * 1024 * 1024


def forward(spread, pieces, weights):
    half, features = weights[0].shape[1:]
    rows = sum(piece.shape[0] for piece in pieces)
    shape = jax.ShapeDtypeStruct
    out_shape = [
        shape((rows, features), jnp.bfloat16),
        shape((rows, 2 * half), jnp.float32),
        shape((rows, 2 * half), jnp.float32),
        shape((rows, UNIT_TILE), jnp.float32),
        shape((rows, 2 * half), jnp.bfloat16),
    ]
    scratch = [pltpu.VMEM((rows, pieces[0].shape[1]), jnp.bfloat16)]
    return products(forward_kernel, "forward_products", spread, pieces, weights, [], out_shape, scratch)


def backward(collect, pieces, weights, *saved):
    half, features = weights[0].shape[1:]
    rows = sum(piece.shape[0] for piece in pieces)
    shape = jax.ShapeDtypeStruct
    out_shape = [
        shape((rows, features), jnp.bfloat16),
        shape((rows, collect.shape[1]), jnp.bfloat16),
        shape((rows, features), jnp.bfloat16),
        shape((half, features), jnp.bfloat16),
    ]
    scratch = [pltpu.VMEM((rows, 2 * half), jnp.bfloat16)] * 2 + [pltpu.VMEM((rows, UNIT_TILE), jnp.float32)]
    return products(backward_kernel, "backward_products", collect, pieces, weights, saved, out_shape, scratch)


def share_kernel(weighted, rows, other, out):
    total = dot_first(weighted[...], rows[...]) + other[...].astype(jnp.float32)
    out[...] = total.astype(jnp.bfloat16).reshape(out.shape)


def finish_share(weighted, rows, other, local_experts):
    count, features = rows.shape
    units = other.shape[0] // local_experts
    tile = UNIT_TILE // local_experts
    return pl.pallas_call(
        share_kernel,
        grid=(units // tile,),
        in_specs=[
            pl.BlockSpec((count, UNIT_TILE), lambda i: (0, i)),
            whole(rows),
            pl.BlockSpec((UNIT_TILE, features), lambda i: (i, 0)),
        ],
        out_specs=pl.BlockSpec((tile, local_experts, features), lambda i: (i, 0, 0)),
        out_shape=jax.ShapeDtypeStruct((units, local_experts, features), jnp.bfloat16),
        compiler_params=pltpu.CompilerParams(**PARAMS),
        cost_estimate=pl.CostEstimate(
            flops=2 * count * other.size, bytes_accessed=4 * other.size, transcendentals=0
        ),
        name="finish_share",
    )(weighted, rows, other)


def local_tokens(tokens, out_grad, expert_ids, slot_pos, combine_weight, w_gate, w_up, w_down):
    units, local_experts, width = w_gate.shape
    experts = local_experts * lax.axis_size("expert")
    first_expert = lax.axis_index("expert") * local_experts
    unit_rows = units * local_experts
    picked = (expert_ids[:, :, None] == jnp.arange(experts, dtype=jnp.int32)) & (slot_pos >= 0)[:, :, None]
    side = -(-2 * experts // 128) * 128
    unit_expert = first_expert + jnp.arange(UNIT_TILE, dtype=jnp.int32) % local_experts
    columns = jnp.arange(side, dtype=jnp.int32)
    spread = (columns[:, None] % experts == unit_expert[None, :]) & (columns < 2 * experts)[:, None]
    collect = (unit_expert[:, None] == columns[None, :]).astype(jnp.bfloat16)
    spread = spread.astype(jnp.bfloat16)

    own_t = payload(tokens, expert_ids, slot_pos, combine_weight, experts, side)
    own_t, own_g, w_gate = lax.optimization_barrier((own_t, out_grad, w_gate))
    column_t = [over_z(own_t, bit) for bit in (2, 1, 3)]
    own_gx = over_dp(own_g, 2)
    weights = merge_units(w_gate, w_up, w_down)
    column_t, own_gx, own_g, weights = lax.optimization_barrier((column_t, own_gx, own_g, weights))

    pieces_t = [own_t, *column_t]
    column_tx = over_dp(jnp.concatenate(pieces_t, axis=0), 2)
    column_g = [over_z(own_g, bit) for bit in (2, 1, 3)]
    weights_b = over_dp(weights, 1)
    column_g, column_tx = lax.optimization_barrier((column_g, column_tx))

    away_gx = over_dp(jnp.concatenate(column_g, axis=0), 2)
    weights = [weights, weights_b]
    out_part, gate_pre, up_pre, mask, weighted = forward(spread, [*pieces_t, column_tx], weights)
    out_part, away_gx = lax.optimization_barrier((out_part, away_gx))

    half = out_part.shape[0] // 2
    pair, block = half // 2, half // 4
    out_x = over_dp(out_part[half:], 2)
    grad_pieces = [out_grad, *column_g, own_gx, away_gx]
    saved = (gate_pre, up_pre, mask, weighted)
    grad_part, product_part, grad_rows, share_b = backward(collect, grad_pieces, weights, *saved)
    grad_part, product_part, out_x, share_b = lax.optimization_barrier((grad_part, product_part, out_x, share_b))

    grad_part = jnp.concatenate([grad_part, product_part], axis=1)
    near_x = over_dp(grad_part[half + pair :], 2)
    out_sum = add(out_part[:half], out_x)
    out_near = over_z(narrow(out_sum[pair:]), 1)
    other_share = over_dp(share_b, 1)
    near_x, out_near = lax.optimization_barrier((near_x, out_near))

    grad_near = over_z(narrow(add(grad_part[pair:half], near_x)), 1)
    pair_x = over_dp(grad_part[half : half + pair], 2)
    out_sum = add(out_sum[:pair], out_near)
    out_far = over_z(narrow(out_sum[block:]), 2)
    grad_near, pair_x, out_far, other_share = lax.optimization_barrier((grad_near, pair_x, out_far, other_share))

    sums = add(add(grad_part[:pair], pair_x), grad_near)
    grad_far = over_z(narrow(sums[block:]), 2)
    layer_out = narrow(add(out_sum[:block], out_far))
    down_grad = finish_share(weighted, grad_rows, other_share, local_experts)
    grad_far, down_grad, layer_out = lax.optimization_barrier((grad_far, down_grad, layer_out))
    sums = add(sums[:block], grad_far)
    input_grad = narrow(sums[:, :width])
    per_expert = sums[:, width : width + experts]
    weight_grad = jnp.sum(jnp.where(picked, per_expert[:, None, :], 0.0), axis=2)
    return (layer_out, input_grad, weight_grad, down_grad)


def plan(tokens, out_grad, expert_ids, slot_pos, combine_weight, w_gate, w_up, w_down):
    args = (tokens, out_grad, expert_ids, slot_pos, combine_weight, w_gate, w_up, w_down)
    slots = tokens.shape[0] * expert_ids.shape[1] // lax.axis_size("expert")
    unit_rows = w_gate.shape[0] * w_gate.shape[1]
    tiled = w_gate.shape[0] % 64 == 0 and unit_rows % UNIT_TILE == 0 and UNIT_TILE % w_gate.shape[1] == 0
    tiled = tiled and w_gate.shape[1] % 2 == 0 and w_gate.shape[2] % WIDTH_TILE == 0 and tokens.shape[0] % 32 == 0
    four = lax.axis_size("expert") == 4 and lax.axis_size("dp") == 4
    if tokens.shape[0] < slots and tiled and four:
        return local_tokens(*args)
    return local(*args)


def solution(mesh):
    in_specs = (
        P(("groups", "expert", "dp"), None),
        P(("groups", "expert", "dp"), None),
        P(("groups", "expert", "dp"), None),
        P(("groups", "expert", "dp"), None),
        P(("groups", "expert", "dp"), None),
        P("dp", "expert", None),
        P("dp", "expert", None),
        P("dp", "expert", None),
    )
    out_specs = (
        P(("groups", "expert", "dp"), None),
        P(("groups", "expert", "dp"), None),
        P(("groups", "expert", "dp"), None),
        P(("groups", "dp"), "expert", None),
    )
    return jax.shard_map(plan, mesh=mesh, in_specs=in_specs, out_specs=out_specs, check_vma=False)
```

```python
import functools

import jax
import jax.numpy as jnp
from jax import lax
from jax.experimental import pallas as pl
from jax.experimental.pallas import tpu as pltpu
from jax.sharding import PartitionSpec as P


def slot_places(expert_ids, slot_pos, local_experts, row_total, capacity):
    flat_place = (
        expert_ids % local_experts * row_total + expert_ids // local_experts * capacity + slot_pos
    )
    return jnp.where(slot_pos >= 0, flat_place, -1)


def local(tokens, out_grad, expert_ids, slot_pos, combine_weight, w_gate, w_up, w_down):
    local_experts = w_gate.shape[1]
    expert_peers = lax.axis_size("expert")
    tok_count = tokens.shape[0]
    top_count = expert_ids.shape[1]
    model_width = tokens.shape[1]
    capacity = tok_count * top_count // (local_experts * expert_peers)
    row_total = expert_peers * capacity
    slot_count = local_experts * row_total
    kept_mask = slot_pos >= 0
    flat_place = slot_places(expert_ids, slot_pos, local_experts, row_total, capacity)
    places = jnp.arange(slot_count, dtype=jnp.int32)
    onehot = (flat_place[:, :, None] == places[None, None, :]).astype(jnp.float32)
    present = jnp.sum(onehot, axis=1)
    weighted = jnp.sum(onehot * combine_weight[:, :, None], axis=1)
    sent_rows = jnp.einsum(
        "tw,td->wd", present.astype(jnp.bfloat16), tokens, preferred_element_type=jnp.float32
    )
    sent_cot = jnp.einsum(
        "tw,td->wd", weighted, out_grad.astype(jnp.float32), precision=lax.Precision.HIGHEST
    )
    sent_rows = sent_rows.astype(jnp.bfloat16).reshape(local_experts, row_total, model_width)
    sent_cot = sent_cot.astype(jnp.bfloat16).reshape(local_experts, row_total, model_width)
    expert_rows, expert_cot = (
        lax.all_to_all(sent_rows, "expert", split_axis=1, concat_axis=1, tiled=True),
        lax.all_to_all(sent_cot, "expert", split_axis=1, concat_axis=1, tiled=True),
    )
    gate_piece = lax.all_gather(w_gate, "dp", axis=0, tiled=True)
    up_piece = lax.all_gather(w_up, "dp", axis=0, tiled=True)
    down_piece = lax.all_gather(w_down, "dp", axis=0, tiled=True)
    gate_pre = jnp.einsum(
        "nld,lrd->lnr", gate_piece, expert_rows, preferred_element_type=jnp.float32
    )
    up_pre = jnp.einsum("nld,lrd->lnr", up_piece, expert_rows, preferred_element_type=jnp.float32)
    sigmoid_val = jax.nn.sigmoid(gate_pre)
    hidden = (gate_pre * sigmoid_val * up_pre).astype(jnp.bfloat16)
    expert_out = jnp.einsum("lnr,nld->lrd", hidden, down_piece, preferred_element_type=jnp.float32)
    hidden_grad = jnp.einsum(
        "nld,lrd->lnr", down_piece, expert_cot, preferred_element_type=jnp.float32
    )
    gate_grad = (
        hidden_grad * up_pre * sigmoid_val * (1.0 + gate_pre * (1.0 - sigmoid_val))
    ).astype(jnp.bfloat16)
    up_grad = (hidden_grad * gate_pre * sigmoid_val).astype(jnp.bfloat16)
    slot_back = jnp.einsum(
        "lnr,nld->lrd", gate_grad, gate_piece, preferred_element_type=jnp.float32
    )
    slot_back = slot_back + jnp.einsum(
        "lnr,nld->lrd", up_grad, up_piece, preferred_element_type=jnp.float32
    )
    hidden_all, expert_out, slot_back = (hidden, expert_out, slot_back)
    back_out, back_grad = (
        lax.all_to_all(
            expert_out.astype(jnp.bfloat16), "expert", split_axis=1, concat_axis=1, tiled=True
        ),
        lax.all_to_all(
            slot_back.astype(jnp.bfloat16), "expert", split_axis=1, concat_axis=1, tiled=True
        ),
    )
    back_out = back_out.reshape(slot_count, model_width)
    back_grad = back_grad.reshape(slot_count, model_width)
    safe_place = jnp.maximum(flat_place, 0)
    picked_out = jnp.where(
        kept_mask[:, :, None], jnp.take(back_out, safe_place, axis=0).astype(jnp.float32), 0.0
    )
    picked_grad = jnp.where(
        kept_mask[:, :, None], jnp.take(back_grad, safe_place, axis=0).astype(jnp.float32), 0.0
    )
    layer_out = jnp.sum(combine_weight[:, :, None] * picked_out, axis=1).astype(jnp.bfloat16)
    input_grad = jnp.sum(picked_grad, axis=1).astype(jnp.bfloat16)
    weight_grad = jnp.sum(picked_out * out_grad.astype(jnp.float32)[:, None, :], axis=2)
    down_grad = lax.psum_scatter(
        jnp.einsum(
            "lnr,lrd->nld", hidden_all, expert_cot, preferred_element_type=jnp.float32
        ).astype(jnp.bfloat16),
        "dp",
        scatter_dimension=0,
        tiled=True,
    )
    return (layer_out, input_grad, weight_grad, down_grad)


def over_z(rows, bit):
    return lax.ppermute(rows, "expert", [(i, i ^ bit) for i in range(lax.axis_size("expert"))])


def over_dp(rows, bit):
    return lax.ppermute(rows, "dp", [(i, i ^ bit) for i in range(lax.axis_size("dp"))])


def add(kept, other):
    return kept.astype(jnp.float32) + other.astype(jnp.float32)


def narrow(rows):
    return rows.astype(jnp.bfloat16)


def dot_last(a, b):
    return lax.dot_general(a, b, (((1,), (1,)), ((), ())), preferred_element_type=jnp.float32)


def dot_plain(a, b):
    return lax.dot_general(a, b, (((1,), (0,)), ((), ())), preferred_element_type=jnp.float32)


def dot_first(a, b):
    return lax.dot_general(a, b, (((0,), (0,)), ((), ())), preferred_element_type=jnp.float32)


UNIT_TILE = 256
WIDTH_TILE = 512


def place_rows(pieces, rows):
    start = 0
    for piece in pieces:
        count = piece.shape[0]
        rows[pl.ds(start, count), :] = piece[...]
        start += count


def payload_kernel(experts, tokens, ids, pos, weights, out):
    picks, count = ids.shape
    expert = lax.broadcasted_iota(jnp.int32, (experts, count), 0)
    weight = jnp.zeros((experts, count), jnp.float32)
    for k in range(picks):
        row = pl.ds(k, 1)
        weight += jnp.where((ids[row, :] == expert) & (pos[row, :] >= 0), weights[row, :], 0.0)
    high = weight.astype(jnp.bfloat16)
    low = (weight - high.astype(jnp.float32)).astype(jnp.bfloat16)
    both = jnp.concatenate([high, low], axis=0)
    width = tokens.shape[1]
    spot = (both.shape[0], out.shape[1] - width)
    same = lax.broadcasted_iota(jnp.int32, spot, 0) == lax.broadcasted_iota(jnp.int32, spot, 1)
    routed = dot_first(both, same.astype(jnp.float32).astype(jnp.bfloat16))
    out[:, :width] = tokens[...]
    out[:, width:] = routed.astype(jnp.bfloat16)


def payload(tokens, ids, pos, weights, experts, side):
    rows, width = tokens.shape
    return pl.pallas_call(
        functools.partial(payload_kernel, experts),
        in_specs=[IN_VMEM] * 4,
        out_specs=IN_VMEM,
        out_shape=jax.ShapeDtypeStruct((rows, width + side), tokens.dtype),
        name="payload",
    )(tokens, ids.T, pos.T, weights.T)


def bring(sources, held, sems, order):
    copies = {}
    for half, slot in order:
        copy = pltpu.make_async_copy(sources[half].at[slot], held[half].at[slot], sems.at[half, slot])
        copy.start()
        copies[half, slot] = copy
    return copies


def unit_tiles(half_rows):
    return [(half, at) for half in range(2) for at in range(0, half_rows, UNIT_TILE)]


def forward_kernel(spread, *refs):
    pieces, (weights_a, weights_b, kept, sent, gate_out, up_out, mask, weighted, rows, held_a, held_b, sems) = refs[:5], refs[5:]
    held = (held_a, held_b)
    order = [(0, 0), (0, 1), (1, 0), (1, 1), (0, 2), (1, 2)]
    copies = bring((weights_a, weights_b), held, sems, order)
    half_rows, features = held_a.shape[1:]
    place_rows(pieces, rows)
    mask[...] = dot_plain(rows[:, features:], spread[...])
    for half, at in unit_tiles(half_rows):
        if at == 0:
            copies[half, 0].wait()
            copies[half, 1].wait()
        units = pl.ds(at, UNIT_TILE)
        gate_pre = dot_last(rows[:, :features], held[half][0, units, :])
        up_pre = dot_last(rows[:, :features], held[half][1, units, :])
        columns = pl.ds(half * half_rows + at, UNIT_TILE)
        gate_out[:, columns] = gate_pre
        up_out[:, columns] = up_pre
        hidden = gate_pre * jax.nn.sigmoid(gate_pre) * up_pre
        weighted[:, columns] = (hidden * mask[...]).astype(jnp.bfloat16)
    copies[0, 2].wait()
    copies[1, 2].wait()
    for at in range(0, features, WIDTH_TILE):
        columns = pl.ds(at, WIDTH_TILE)
        total = dot_plain(weighted[:, :half_rows], held_a[2, :, columns])
        total += dot_plain(weighted[:, half_rows:], held_b[2, :, columns])
        spread_out(total, (kept, sent), at, WIDTH_TILE)


def spread_out(total, outs, at, width):
    start = 0
    for out in outs:
        count = out.shape[0]
        out[:, pl.ds(at, width)] = total[start : start + count].astype(jnp.bfloat16)
        start += count


def backward_kernel(collect, *refs):
    pieces, refs = refs[:6], refs[6:]
    weights_a, weights_b, gate_in, up_in, mask, weighted, kept, pair_out, near_out, rows, share, gate_grad, up_grad, product, held_a, held_b, sems = refs
    held = (held_a, held_b)
    order = [(0, 2), (1, 2), (0, 0), (1, 0), (0, 1), (1, 1)]
    copies = bring((weights_a, weights_b), held, sems, order)
    half_rows, features = held_a.shape[1:]
    place_rows(pieces, rows)
    for half, at in unit_tiles(half_rows):
        if at == 0:
            copies[half, 2].wait()
        hidden_grad = dot_last(rows[...], held[half][2, pl.ds(at, UNIT_TILE), :])
        columns = pl.ds(half * half_rows + at, UNIT_TILE)
        gate_pre, up_pre, weight = gate_in[:, columns], up_in[:, columns], mask[...]
        sig = jax.nn.sigmoid(gate_pre)
        gate_sig = gate_pre * sig
        term = jnp.where(weight > 0, gate_sig * up_pre * hidden_grad, 0.0)
        product[...] = term if half == 0 and at == 0 else product[...] + term
        hidden_grad = hidden_grad * weight
        slope = sig * (1.0 + gate_pre * (1.0 - sig))
        gate_grad[:, columns] = (hidden_grad * up_pre * slope).astype(jnp.bfloat16)
        up_grad[:, columns] = (hidden_grad * gate_sig).astype(jnp.bfloat16)
    outs = (kept, pair_out, near_out)
    spread_out(dot_plain(product[...].astype(jnp.bfloat16), collect[...]), outs, features, kept.shape[1] - features)
    for at in range(0, half_rows, UNIT_TILE):
        part = dot_first(weighted[:, pl.ds(half_rows + at, UNIT_TILE)], rows[...])
        share[pl.ds(at, UNIT_TILE), :] = part.astype(jnp.bfloat16)
    for half, slot in order[2:]:
        copies[half, slot].wait()
    for at in range(0, features, WIDTH_TILE):
        columns = pl.ds(at, WIDTH_TILE)
        total = dot_plain(gate_grad[:, :half_rows], held_a[0, :, columns])
        total += dot_plain(gate_grad[:, half_rows:], held_b[0, :, columns])
        total += dot_plain(up_grad[:, :half_rows], held_a[1, :, columns])
        total += dot_plain(up_grad[:, half_rows:], held_b[1, :, columns])
        spread_out(total, outs, at, WIDTH_TILE)


def merge_kernel(gate, up, down, merged):
    for slot, part in enumerate((gate, up, down)):
        merged[slot] = part[...].reshape(merged.shape[1:])


def merge_units(gate, up, down):
    units, experts, features = gate.shape
    tile = 32
    block = pl.BlockSpec((tile, experts, features), lambda i: (i, 0, 0))
    return pl.pallas_call(
        merge_kernel,
        grid=(units // tile,),
        in_specs=[block] * 3,
        out_specs=pl.BlockSpec((3, tile * experts, features), lambda i: (0, i, 0)),
        out_shape=jax.ShapeDtypeStruct((3, units * experts, features), gate.dtype),
        compiler_params=pltpu.CompilerParams(**PARAMS),
        cost_estimate=pl.CostEstimate(flops=0, bytes_accessed=12 * gate.size, transcendentals=0),
        name="merge_units",
    )(gate, up, down)


def whole(array):
    return pl.BlockSpec(array.shape, lambda i: (0, 0))


def cost(rows, units, features, products):
    return pl.CostEstimate(
        flops=2 * rows * units * features * products,
        bytes_accessed=6 * units * features + 4 * rows * features,
        transcendentals=rows * units,
    )


PARAMS = dict(dimension_semantics=("arbitrary",), vmem_limit_bytes=24 * 1024 * 1024)
IN_VMEM = pl.BlockSpec(memory_space=pltpu.VMEM)


def products(kernel, name, table, pieces, weights, saved, out_shape, scratch):
    half, features = weights[0].shape[1:]
    rows = sum(piece.shape[0] for piece in pieces)
    held = [pltpu.VMEM(w.shape, w.dtype) for w in weights]
    return pl.pallas_call(
        kernel,
        in_specs=[IN_VMEM] * (1 + len(pieces)) + [pl.BlockSpec(memory_space=pl.ANY)] * 2 + [IN_VMEM] * len(saved),
        out_specs=[IN_VMEM] * len(out_shape),
        out_shape=out_shape,
        scratch_shapes=[*scratch, *held, pltpu.SemaphoreType.DMA((2, 3))],
        compiler_params=pltpu.CompilerParams(vmem_limit_bytes=PRODUCT_VMEM),
        cost_estimate=cost(rows, 2 * half, features, 3),
        name=name,
    )(table, *pieces, *weights, *saved)


PRODUCT_VMEM = 34 * 1024 * 1024


def forward(spread, pieces, weights):
    half, features = weights[0].shape[1:]
    rows = sum(piece.shape[0] for piece in pieces)
    shape = jax.ShapeDtypeStruct
    out_shape = [
        shape((rows // 2, features), jnp.bfloat16),
        shape((rows // 2, features), jnp.bfloat16),
        shape((rows, 2 * half), jnp.float32),
        shape((rows, 2 * half), jnp.float32),
        shape((rows, UNIT_TILE), jnp.float32),
        shape((rows, 2 * half), jnp.bfloat16),
    ]
    scratch = [pltpu.VMEM((rows, pieces[0].shape[1]), jnp.bfloat16)]
    return products(forward_kernel, "forward_products", spread, pieces, weights, [], out_shape, scratch)


def backward(collect, pieces, weights, *saved):
    half, features = weights[0].shape[1:]
    rows = sum(piece.shape[0] for piece in pieces)
    shape = jax.ShapeDtypeStruct
    out_shape = [
        shape((rows // 2, features + collect.shape[1]), jnp.bfloat16),
        shape((rows // 4, features + collect.shape[1]), jnp.bfloat16),
        shape((rows // 4, features + collect.shape[1]), jnp.bfloat16),
        shape((rows, features), jnp.bfloat16),
        shape((half, features), jnp.bfloat16),
    ]
    scratch = [pltpu.VMEM((rows, 2 * half), jnp.bfloat16)] * 2 + [pltpu.VMEM((rows, UNIT_TILE), jnp.float32)]
    return products(backward_kernel, "backward_products", collect, pieces, weights, saved, out_shape, scratch)


def share_kernel(weighted, rows, other, out):
    total = dot_first(weighted[...], rows[...]) + other[...].astype(jnp.float32)
    out[...] = total.astype(jnp.bfloat16).reshape(out.shape)


def finish_share(weighted, rows, other, local_experts):
    count, features = rows.shape
    units = other.shape[0] // local_experts
    tile = UNIT_TILE // local_experts
    return pl.pallas_call(
        share_kernel,
        grid=(units // tile,),
        in_specs=[
            pl.BlockSpec((count, UNIT_TILE), lambda i: (0, i)),
            whole(rows),
            pl.BlockSpec((UNIT_TILE, features), lambda i: (i, 0)),
        ],
        out_specs=pl.BlockSpec((tile, local_experts, features), lambda i: (i, 0, 0)),
        out_shape=jax.ShapeDtypeStruct((units, local_experts, features), jnp.bfloat16),
        compiler_params=pltpu.CompilerParams(**PARAMS),
        cost_estimate=pl.CostEstimate(
            flops=2 * count * other.size, bytes_accessed=4 * other.size, transcendentals=0
        ),
        name="finish_share",
    )(weighted, rows, other)


def local_tokens(tokens, out_grad, expert_ids, slot_pos, combine_weight, w_gate, w_up, w_down):
    units, local_experts, width = w_gate.shape
    experts = local_experts * lax.axis_size("expert")
    first_expert = lax.axis_index("expert") * local_experts
    unit_rows = units * local_experts
    picked = (expert_ids[:, :, None] == jnp.arange(experts, dtype=jnp.int32)) & (slot_pos >= 0)[:, :, None]
    side = -(-2 * experts // 128) * 128
    unit_expert = first_expert + jnp.arange(UNIT_TILE, dtype=jnp.int32) % local_experts
    columns = jnp.arange(side, dtype=jnp.int32)
    spread = (columns[:, None] % experts == unit_expert[None, :]) & (columns < 2 * experts)[:, None]
    collect = (unit_expert[:, None] == columns[None, :]).astype(jnp.bfloat16)
    spread = spread.astype(jnp.bfloat16)

    own_t = payload(tokens, expert_ids, slot_pos, combine_weight, experts, side)
    own_t, own_g, w_gate = lax.optimization_barrier((own_t, out_grad, w_gate))
    column_t = [over_z(own_t, bit) for bit in (2, 1, 3)]
    own_gx = over_dp(own_g, 2)
    weights = merge_units(w_gate, w_up, w_down)
    column_t, own_gx, own_g, weights = lax.optimization_barrier((column_t, own_gx, own_g, weights))

    pieces_t = [own_t, *column_t]
    column_tx = over_dp(jnp.concatenate(pieces_t, axis=0), 2)
    column_g = [over_z(own_g, bit) for bit in (2, 1, 3)]
    weights_b = over_dp(weights, 1)
    column_g, column_tx = lax.optimization_barrier((column_g, column_tx))

    away_gx = over_dp(jnp.concatenate(column_g, axis=0), 2)
    weights = [weights, weights_b]
    out_kept, out_sent, gate_pre, up_pre, mask, weighted = forward(spread, [*pieces_t, column_tx], weights)
    out_sent, away_gx = lax.optimization_barrier((out_sent, away_gx))

    block = tokens.shape[0]
    pair = 2 * block
    out_x = over_dp(out_sent, 2)
    grad_pieces = [out_grad, *column_g, own_gx, away_gx]
    saved = (gate_pre, up_pre, mask, weighted)
    kept, pair_sent, near_sent, grad_rows, share_b = backward(collect, grad_pieces, weights, *saved)
    near_sent, out_x, share_b = lax.optimization_barrier((near_sent, out_x, share_b))

    near_x = over_dp(near_sent, 2)
    out_sum = add(out_kept, out_x)
    out_near = over_z(narrow(out_sum[pair:]), 1)
    other_share = over_dp(share_b, 1)
    near_x, pair_sent = lax.optimization_barrier((near_x, pair_sent))

    grad_near = over_z(narrow(add(kept[pair:], near_x)), 1)
    pair_x = over_dp(pair_sent, 2)
    out_sum = add(out_sum[:pair], out_near)
    out_far = over_z(narrow(out_sum[block:]), 2)
    grad_near, pair_x, out_far, other_share = lax.optimization_barrier((grad_near, pair_x, out_far, other_share))

    sums = add(add(kept[:pair], pair_x), grad_near)
    grad_far = over_z(narrow(sums[block:]), 2)
    layer_out = narrow(add(out_sum[:block], out_far))
    down_grad = finish_share(weighted, grad_rows, other_share, local_experts)
    grad_far, down_grad, layer_out = lax.optimization_barrier((grad_far, down_grad, layer_out))
    sums = add(sums[:block], grad_far)
    input_grad = narrow(sums[:, :width])
    per_expert = sums[:, width : width + experts]
    weight_grad = jnp.sum(jnp.where(picked, per_expert[:, None, :], 0.0), axis=2)
    return (layer_out, input_grad, weight_grad, down_grad)


def plan(tokens, out_grad, expert_ids, slot_pos, combine_weight, w_gate, w_up, w_down):
    args = (tokens, out_grad, expert_ids, slot_pos, combine_weight, w_gate, w_up, w_down)
    slots = tokens.shape[0] * expert_ids.shape[1] // lax.axis_size("expert")
    unit_rows = w_gate.shape[0] * w_gate.shape[1]
    tiled = w_gate.shape[0] % 64 == 0 and unit_rows % UNIT_TILE == 0 and UNIT_TILE % w_gate.shape[1] == 0
    tiled = tiled and w_gate.shape[1] % 2 == 0 and w_gate.shape[2] % WIDTH_TILE == 0 and tokens.shape[0] % 32 == 0
    four = lax.axis_size("expert") == 4 and lax.axis_size("dp") == 4
    if tokens.shape[0] < slots and tiled and four:
        return local_tokens(*args)
    return local(*args)


def solution(mesh):
    in_specs = (
        P(("groups", "expert", "dp"), None),
        P(("groups", "expert", "dp"), None),
        P(("groups", "expert", "dp"), None),
        P(("groups", "expert", "dp"), None),
        P(("groups", "expert", "dp"), None),
        P("dp", "expert", None),
        P("dp", "expert", None),
        P("dp", "expert", None),
    )
    out_specs = (
        P(("groups", "expert", "dp"), None),
        P(("groups", "expert", "dp"), None),
        P(("groups", "expert", "dp"), None),
        P(("groups", "dp"), "expert", None),
    )
    return jax.shard_map(plan, mesh=mesh, in_specs=in_specs, out_specs=out_specs, check_vma=False)
```

```python
import functools

import jax
import jax.numpy as jnp
from jax import lax
from jax.experimental import pallas as pl
from jax.experimental.pallas import tpu as pltpu
from jax.sharding import PartitionSpec as P


def slot_places(expert_ids, slot_pos, local_experts, row_total, capacity):
    flat_place = (
        expert_ids % local_experts * row_total + expert_ids // local_experts * capacity + slot_pos
    )
    return jnp.where(slot_pos >= 0, flat_place, -1)


def local(tokens, out_grad, expert_ids, slot_pos, combine_weight, w_gate, w_up, w_down):
    local_experts = w_gate.shape[1]
    expert_peers = lax.axis_size("expert")
    tok_count = tokens.shape[0]
    top_count = expert_ids.shape[1]
    model_width = tokens.shape[1]
    capacity = tok_count * top_count // (local_experts * expert_peers)
    row_total = expert_peers * capacity
    slot_count = local_experts * row_total
    kept_mask = slot_pos >= 0
    flat_place = slot_places(expert_ids, slot_pos, local_experts, row_total, capacity)
    places = jnp.arange(slot_count, dtype=jnp.int32)
    onehot = (flat_place[:, :, None] == places[None, None, :]).astype(jnp.float32)
    present = jnp.sum(onehot, axis=1)
    weighted = jnp.sum(onehot * combine_weight[:, :, None], axis=1)
    sent_rows = jnp.einsum(
        "tw,td->wd", present.astype(jnp.bfloat16), tokens, preferred_element_type=jnp.float32
    )
    sent_cot = jnp.einsum(
        "tw,td->wd", weighted, out_grad.astype(jnp.float32), precision=lax.Precision.HIGHEST
    )
    sent_rows = sent_rows.astype(jnp.bfloat16).reshape(local_experts, row_total, model_width)
    sent_cot = sent_cot.astype(jnp.bfloat16).reshape(local_experts, row_total, model_width)
    expert_rows, expert_cot = (
        lax.all_to_all(sent_rows, "expert", split_axis=1, concat_axis=1, tiled=True),
        lax.all_to_all(sent_cot, "expert", split_axis=1, concat_axis=1, tiled=True),
    )
    gate_piece = lax.all_gather(w_gate, "dp", axis=0, tiled=True)
    up_piece = lax.all_gather(w_up, "dp", axis=0, tiled=True)
    down_piece = lax.all_gather(w_down, "dp", axis=0, tiled=True)
    gate_pre = jnp.einsum(
        "nld,lrd->lnr", gate_piece, expert_rows, preferred_element_type=jnp.float32
    )
    up_pre = jnp.einsum("nld,lrd->lnr", up_piece, expert_rows, preferred_element_type=jnp.float32)
    sigmoid_val = jax.nn.sigmoid(gate_pre)
    hidden = (gate_pre * sigmoid_val * up_pre).astype(jnp.bfloat16)
    expert_out = jnp.einsum("lnr,nld->lrd", hidden, down_piece, preferred_element_type=jnp.float32)
    hidden_grad = jnp.einsum(
        "nld,lrd->lnr", down_piece, expert_cot, preferred_element_type=jnp.float32
    )
    gate_grad = (
        hidden_grad * up_pre * sigmoid_val * (1.0 + gate_pre * (1.0 - sigmoid_val))
    ).astype(jnp.bfloat16)
    up_grad = (hidden_grad * gate_pre * sigmoid_val).astype(jnp.bfloat16)
    slot_back = jnp.einsum(
        "lnr,nld->lrd", gate_grad, gate_piece, preferred_element_type=jnp.float32
    )
    slot_back = slot_back + jnp.einsum(
        "lnr,nld->lrd", up_grad, up_piece, preferred_element_type=jnp.float32
    )
    hidden_all, expert_out, slot_back = (hidden, expert_out, slot_back)
    back_out, back_grad = (
        lax.all_to_all(
            expert_out.astype(jnp.bfloat16), "expert", split_axis=1, concat_axis=1, tiled=True
        ),
        lax.all_to_all(
            slot_back.astype(jnp.bfloat16), "expert", split_axis=1, concat_axis=1, tiled=True
        ),
    )
    back_out = back_out.reshape(slot_count, model_width)
    back_grad = back_grad.reshape(slot_count, model_width)
    safe_place = jnp.maximum(flat_place, 0)
    picked_out = jnp.where(
        kept_mask[:, :, None], jnp.take(back_out, safe_place, axis=0).astype(jnp.float32), 0.0
    )
    picked_grad = jnp.where(
        kept_mask[:, :, None], jnp.take(back_grad, safe_place, axis=0).astype(jnp.float32), 0.0
    )
    layer_out = jnp.sum(combine_weight[:, :, None] * picked_out, axis=1).astype(jnp.bfloat16)
    input_grad = jnp.sum(picked_grad, axis=1).astype(jnp.bfloat16)
    weight_grad = jnp.sum(picked_out * out_grad.astype(jnp.float32)[:, None, :], axis=2)
    down_grad = lax.psum_scatter(
        jnp.einsum(
            "lnr,lrd->nld", hidden_all, expert_cot, preferred_element_type=jnp.float32
        ).astype(jnp.bfloat16),
        "dp",
        scatter_dimension=0,
        tiled=True,
    )
    return (layer_out, input_grad, weight_grad, down_grad)


def over_z(rows, bit):
    return lax.ppermute(rows, "expert", [(i, i ^ bit) for i in range(lax.axis_size("expert"))])


def over_dp(rows, bit):
    return lax.ppermute(rows, "dp", [(i, i ^ bit) for i in range(lax.axis_size("dp"))])


def add(kept, other):
    return kept.astype(jnp.float32) + other.astype(jnp.float32)


def narrow(rows):
    return rows.astype(jnp.bfloat16)


def dot_last(a, b):
    return lax.dot_general(a, b, (((1,), (1,)), ((), ())), preferred_element_type=jnp.float32)


def dot_plain(a, b):
    return lax.dot_general(a, b, (((1,), (0,)), ((), ())), preferred_element_type=jnp.float32)


def dot_first(a, b):
    return lax.dot_general(a, b, (((0,), (0,)), ((), ())), preferred_element_type=jnp.float32)


UNIT_TILE = 256
WIDTH_TILE = 512


def place_rows(pieces, rows):
    start = 0
    for piece in pieces:
        count = piece.shape[0]
        rows[pl.ds(start, count), :] = piece[...]
        start += count


def payload_kernel(experts, tokens, ids, pos, weights, out):
    picks, count = ids.shape
    expert = lax.broadcasted_iota(jnp.int32, (experts, count), 0)
    weight = jnp.zeros((experts, count), jnp.float32)
    for k in range(picks):
        row = pl.ds(k, 1)
        weight += jnp.where((ids[row, :] == expert) & (pos[row, :] >= 0), weights[row, :], 0.0)
    high = weight.astype(jnp.bfloat16)
    low = (weight - high.astype(jnp.float32)).astype(jnp.bfloat16)
    both = jnp.concatenate([high, low], axis=0)
    width = tokens.shape[1]
    spot = (both.shape[0], out.shape[1] - width)
    same = lax.broadcasted_iota(jnp.int32, spot, 0) == lax.broadcasted_iota(jnp.int32, spot, 1)
    routed = dot_first(both, same.astype(jnp.float32).astype(jnp.bfloat16))
    out[:, :width] = tokens[...]
    out[:, width:] = routed.astype(jnp.bfloat16)


def payload(tokens, ids, pos, weights, experts, side):
    rows, width = tokens.shape
    return pl.pallas_call(
        functools.partial(payload_kernel, experts),
        in_specs=[IN_VMEM] * 4,
        out_specs=IN_VMEM,
        out_shape=jax.ShapeDtypeStruct((rows, width + side), tokens.dtype),
        name="payload",
    )(tokens, ids.T, pos.T, weights.T)


def bring(sources, held, sems, order):
    copies = {}
    for half, slot in order:
        copy = pltpu.make_async_copy(sources[half].at[slot], held[half].at[slot], sems.at[half, slot])
        copy.start()
        copies[half, slot] = copy
    return copies


def unit_tiles(half_rows):
    return [(half, at) for half in range(2) for at in range(0, half_rows, UNIT_TILE)]


def forward_kernel(spread, *refs):
    pieces, (weights_a, weights_b, kept, sent, gate_out, up_out, mask, weighted, rows, held_a, held_b, sems) = refs[:5], refs[5:]
    held = (held_a, held_b)
    order = [(0, 0), (0, 1), (1, 0), (1, 1), (0, 2), (1, 2)]
    copies = bring((weights_a, weights_b), held, sems, order)
    half_rows, features = held_a.shape[1:]
    place_rows(pieces, rows)
    mask[...] = dot_plain(rows[:, features:], spread[...])
    for half, at in unit_tiles(half_rows):
        if at == 0:
            copies[half, 0].wait()
            copies[half, 1].wait()
        units = pl.ds(at, UNIT_TILE)
        gate_pre = dot_last(rows[:, :features], held[half][0, units, :])
        up_pre = dot_last(rows[:, :features], held[half][1, units, :])
        columns = pl.ds(half * half_rows + at, UNIT_TILE)
        gate_out[:, columns] = gate_pre
        up_out[:, columns] = up_pre
        hidden = gate_pre * jax.nn.sigmoid(gate_pre) * up_pre
        weighted[:, columns] = (hidden * mask[...]).astype(jnp.bfloat16)
    copies[0, 2].wait()
    copies[1, 2].wait()
    for at in range(0, features, WIDTH_TILE):
        columns = pl.ds(at, WIDTH_TILE)
        total = dot_plain(weighted[:, :half_rows], held_a[2, :, columns])
        total += dot_plain(weighted[:, half_rows:], held_b[2, :, columns])
        spread_out(total, (kept, sent), at, WIDTH_TILE)


def spread_out(total, outs, at, width):
    start = 0
    for out in outs:
        count = out.shape[0]
        out[:, pl.ds(at, width)] = total[start : start + count].astype(jnp.bfloat16)
        start += count


def backward_kernel(collect, *refs):
    pieces, refs = refs[:6], refs[6:]
    weights_a, weights_b, gate_in, up_in, mask, weighted, kept, pair_out, near_out, rows, share, gate_grad, up_grad, product, held_a, held_b, sems = refs
    held = (held_a, held_b)
    order = [(0, 2), (1, 2), (0, 0), (1, 0), (0, 1), (1, 1)]
    copies = bring((weights_a, weights_b), held, sems, order)
    half_rows, features = held_a.shape[1:]
    place_rows(pieces, rows)
    for half, at in unit_tiles(half_rows):
        if at == 0:
            copies[half, 2].wait()
        hidden_grad = dot_last(rows[...], held[half][2, pl.ds(at, UNIT_TILE), :])
        columns = pl.ds(half * half_rows + at, UNIT_TILE)
        gate_pre, up_pre, weight = gate_in[:, columns], up_in[:, columns], mask[...]
        sig = jax.nn.sigmoid(gate_pre)
        gate_sig = gate_pre * sig
        term = jnp.where(weight > 0, gate_sig * up_pre * hidden_grad, 0.0)
        product[...] = term if half == 0 and at == 0 else product[...] + term
        hidden_grad = hidden_grad * weight
        slope = sig * (1.0 + gate_pre * (1.0 - sig))
        gate_grad[:, columns] = (hidden_grad * up_pre * slope).astype(jnp.bfloat16)
        up_grad[:, columns] = (hidden_grad * gate_sig).astype(jnp.bfloat16)
    outs = (kept, pair_out, near_out)
    spread_out(dot_plain(product[...].astype(jnp.bfloat16), collect[...]), outs, features, kept.shape[1] - features)
    for at in range(0, half_rows, UNIT_TILE):
        part = dot_first(weighted[:, pl.ds(half_rows + at, UNIT_TILE)], rows[...])
        share[pl.ds(at, UNIT_TILE), :] = part.astype(jnp.bfloat16)
    for half, slot in order[2:]:
        copies[half, slot].wait()
    for at in range(0, features, WIDTH_TILE):
        columns = pl.ds(at, WIDTH_TILE)
        total = dot_plain(gate_grad[:, :half_rows], held_a[0, :, columns])
        total += dot_plain(gate_grad[:, half_rows:], held_b[0, :, columns])
        total += dot_plain(up_grad[:, :half_rows], held_a[1, :, columns])
        total += dot_plain(up_grad[:, half_rows:], held_b[1, :, columns])
        spread_out(total, outs, at, WIDTH_TILE)


def merge_kernel(gate, up, down, merged):
    for slot, part in enumerate((gate, up, down)):
        merged[slot] = part[...].reshape(merged.shape[1:])


def merge_units(gate, up, down):
    units, experts, features = gate.shape
    tile = 32
    block = pl.BlockSpec((tile, experts, features), lambda i: (i, 0, 0))
    return pl.pallas_call(
        merge_kernel,
        grid=(units // tile,),
        in_specs=[block] * 3,
        out_specs=pl.BlockSpec((3, tile * experts, features), lambda i: (0, i, 0)),
        out_shape=jax.ShapeDtypeStruct((3, units * experts, features), gate.dtype),
        compiler_params=pltpu.CompilerParams(**PARAMS),
        cost_estimate=pl.CostEstimate(flops=0, bytes_accessed=12 * gate.size, transcendentals=0),
        name="merge_units",
    )(gate, up, down)


def whole(array):
    return pl.BlockSpec(array.shape, lambda i: (0, 0))


def cost(rows, units, features, products):
    return pl.CostEstimate(
        flops=2 * rows * units * features * products,
        bytes_accessed=6 * units * features + 4 * rows * features,
        transcendentals=rows * units,
    )


PARAMS = dict(dimension_semantics=("arbitrary",), vmem_limit_bytes=24 * 1024 * 1024)
IN_VMEM = pl.BlockSpec(memory_space=pltpu.VMEM)


def products(kernel, name, table, pieces, weights, saved, out_shape, scratch):
    half, features = weights[0].shape[1:]
    rows = sum(piece.shape[0] for piece in pieces)
    held = [pltpu.VMEM(w.shape, w.dtype) for w in weights]
    return pl.pallas_call(
        kernel,
        in_specs=[IN_VMEM] * (1 + len(pieces)) + [pl.BlockSpec(memory_space=pl.ANY)] * 2 + [IN_VMEM] * len(saved),
        out_specs=[IN_VMEM] * len(out_shape),
        out_shape=out_shape,
        scratch_shapes=[*scratch, *held, pltpu.SemaphoreType.DMA((2, 3))],
        compiler_params=pltpu.CompilerParams(vmem_limit_bytes=PRODUCT_VMEM),
        cost_estimate=cost(rows, 2 * half, features, 3),
        name=name,
    )(table, *pieces, *weights, *saved)


PRODUCT_VMEM = 34 * 1024 * 1024


def forward(spread, pieces, weights):
    half, features = weights[0].shape[1:]
    rows = sum(piece.shape[0] for piece in pieces)
    shape = jax.ShapeDtypeStruct
    out_shape = [
        shape((rows // 2, features), jnp.bfloat16),
        shape((rows // 2, features), jnp.bfloat16),
        shape((rows, 2 * half), jnp.float32),
        shape((rows, 2 * half), jnp.float32),
        shape((rows, UNIT_TILE), jnp.float32),
        shape((rows, 2 * half), jnp.bfloat16),
    ]
    scratch = [pltpu.VMEM((rows, pieces[0].shape[1]), jnp.bfloat16)]
    return products(forward_kernel, "forward_products", spread, pieces, weights, [], out_shape, scratch)


def backward(collect, pieces, weights, *saved):
    half, features = weights[0].shape[1:]
    rows = sum(piece.shape[0] for piece in pieces)
    shape = jax.ShapeDtypeStruct
    out_shape = [
        shape((rows // 2, features + collect.shape[1]), jnp.bfloat16),
        shape((rows // 4, features + collect.shape[1]), jnp.bfloat16),
        shape((rows // 4, features + collect.shape[1]), jnp.bfloat16),
        shape((rows, features), jnp.bfloat16),
        shape((half, features), jnp.bfloat16),
    ]
    scratch = [pltpu.VMEM((rows, 2 * half), jnp.bfloat16)] * 2 + [pltpu.VMEM((rows, UNIT_TILE), jnp.float32)]
    return products(backward_kernel, "backward_products", collect, pieces, weights, saved, out_shape, scratch)


def share_kernel(weighted, rows, other, out):
    total = dot_first(weighted[...], rows[...]) + other[...].astype(jnp.float32)
    out[...] = total.astype(jnp.bfloat16).reshape(out.shape)


def finish_share(weighted, rows, other, local_experts):
    count, features = rows.shape
    units = other.shape[0] // local_experts
    tile = UNIT_TILE // local_experts
    return pl.pallas_call(
        share_kernel,
        grid=(units // tile,),
        in_specs=[
            pl.BlockSpec((count, UNIT_TILE), lambda i: (0, i)),
            whole(rows),
            pl.BlockSpec((UNIT_TILE, features), lambda i: (i, 0)),
        ],
        out_specs=pl.BlockSpec((tile, local_experts, features), lambda i: (i, 0, 0)),
        out_shape=jax.ShapeDtypeStruct((units, local_experts, features), jnp.bfloat16),
        compiler_params=pltpu.CompilerParams(**PARAMS),
        cost_estimate=pl.CostEstimate(
            flops=2 * count * other.size, bytes_accessed=4 * other.size, transcendentals=0
        ),
        name="finish_share",
    )(weighted, rows, other)


def local_tokens(tokens, out_grad, expert_ids, slot_pos, combine_weight, w_gate, w_up, w_down):
    units, local_experts, width = w_gate.shape
    experts = local_experts * lax.axis_size("expert")
    first_expert = lax.axis_index("expert") * local_experts
    unit_rows = units * local_experts
    picked = (expert_ids[:, :, None] == jnp.arange(experts, dtype=jnp.int32)) & (slot_pos >= 0)[:, :, None]
    side = -(-2 * experts // 128) * 128
    unit_expert = first_expert + jnp.arange(UNIT_TILE, dtype=jnp.int32) % local_experts
    columns = jnp.arange(side, dtype=jnp.int32)
    spread = (columns[:, None] % experts == unit_expert[None, :]) & (columns < 2 * experts)[:, None]
    collect = (unit_expert[:, None] == columns[None, :]).astype(jnp.bfloat16)
    spread = spread.astype(jnp.bfloat16)

    own_t = payload(tokens, expert_ids, slot_pos, combine_weight, experts, side)
    own_t, own_g = lax.optimization_barrier((own_t, out_grad))
    across = {bit: over_z(own_t, bit) for bit in (3, 2, 1)}
    column_t = [across[bit] for bit in (2, 1, 3)]
    own_gx = over_dp(own_g, 2)
    weights = merge_units(w_gate, w_up, w_down)
    column_t, own_gx, own_g, weights = lax.optimization_barrier((column_t, own_gx, own_g, weights))

    pieces_t = [own_t, *column_t]
    column_tx = over_dp(jnp.concatenate(pieces_t, axis=0), 2)
    across = {bit: over_z(own_g, bit) for bit in (3, 2, 1)}
    column_g = [across[bit] for bit in (2, 1, 3)]
    weights_b = over_dp(weights, 1)
    column_g, column_tx = lax.optimization_barrier((column_g, column_tx))

    away_gx = over_dp(jnp.concatenate(column_g, axis=0), 2)
    weights = [weights, weights_b]
    out_kept, out_sent, gate_pre, up_pre, mask, weighted = forward(spread, [*pieces_t, column_tx], weights)
    out_sent, away_gx = lax.optimization_barrier((out_sent, away_gx))

    block = tokens.shape[0]
    pair = 2 * block
    out_x = over_dp(out_sent, 2)
    grad_pieces = [out_grad, *column_g, own_gx, away_gx]
    saved = (gate_pre, up_pre, mask, weighted)
    kept, pair_sent, near_sent, grad_rows, share_b = backward(collect, grad_pieces, weights, *saved)
    near_sent, out_x, share_b = lax.optimization_barrier((near_sent, out_x, share_b))

    near_x = over_dp(near_sent, 2)
    out_sum = add(out_kept, out_x)
    out_near = over_z(narrow(out_sum[pair:]), 1)
    other_share = over_dp(share_b, 1)
    near_x, pair_sent = lax.optimization_barrier((near_x, pair_sent))

    grad_near = over_z(narrow(add(kept[pair:], near_x)), 1)
    pair_x = over_dp(pair_sent, 2)
    out_sum = add(out_sum[:pair], out_near)
    out_far = over_z(narrow(out_sum[block:]), 2)
    grad_near, pair_x, out_far, other_share = lax.optimization_barrier((grad_near, pair_x, out_far, other_share))

    sums = add(add(kept[:pair], pair_x), grad_near)
    grad_far = over_z(narrow(sums[block:]), 2)
    layer_out = narrow(add(out_sum[:block], out_far))
    down_grad = finish_share(weighted, grad_rows, other_share, local_experts)
    grad_far, down_grad, layer_out = lax.optimization_barrier((grad_far, down_grad, layer_out))
    sums = add(sums[:block], grad_far)
    input_grad = narrow(sums[:, :width])
    per_expert = sums[:, width : width + experts]
    weight_grad = jnp.sum(jnp.where(picked, per_expert[:, None, :], 0.0), axis=2)
    return (layer_out, input_grad, weight_grad, down_grad)


def plan(tokens, out_grad, expert_ids, slot_pos, combine_weight, w_gate, w_up, w_down):
    args = (tokens, out_grad, expert_ids, slot_pos, combine_weight, w_gate, w_up, w_down)
    slots = tokens.shape[0] * expert_ids.shape[1] // lax.axis_size("expert")
    unit_rows = w_gate.shape[0] * w_gate.shape[1]
    tiled = w_gate.shape[0] % 64 == 0 and unit_rows % UNIT_TILE == 0 and UNIT_TILE % w_gate.shape[1] == 0
    tiled = tiled and w_gate.shape[1] % 2 == 0 and w_gate.shape[2] % WIDTH_TILE == 0 and tokens.shape[0] % 32 == 0
    four = lax.axis_size("expert") == 4 and lax.axis_size("dp") == 4
    if tokens.shape[0] < slots and tiled and four:
        return local_tokens(*args)
    return local(*args)


def solution(mesh):
    in_specs = (
        P(("groups", "expert", "dp"), None),
        P(("groups", "expert", "dp"), None),
        P(("groups", "expert", "dp"), None),
        P(("groups", "expert", "dp"), None),
        P(("groups", "expert", "dp"), None),
        P("dp", "expert", None),
        P("dp", "expert", None),
        P("dp", "expert", None),
    )
    out_specs = (
        P(("groups", "expert", "dp"), None),
        P(("groups", "expert", "dp"), None),
        P(("groups", "expert", "dp"), None),
        P(("groups", "dp"), "expert", None),
    )
    return jax.shard_map(plan, mesh=mesh, in_specs=in_specs, out_specs=out_specs, check_vma=False)
```
